32 devices in a mesh: pp: 2 (over y), fsdp: 16 (over z, x, core).
Axes of the slice: x: 2, y: 2, z: 4, core: 2. Of those that a mesh axis runs over, the one named last changes fastest.
Arguments:
- inputs: bfloat16 [2, 2048, 2048], P(None, 'fsdp'), may hold values from -6 to 6
- cotangent: bfloat16 [2, 2048, 2048], P(None, 'fsdp'), may hold values from -0.125 to 0.125
- gains: bfloat16 [2, 2048], P('pp', 'fsdp'), may hold values from 0.5 to 1.5
- w_qkv: bfloat16 [2, 2048, 1536], P('pp', 'fsdp'), may hold values from -0.125 to 0.125
- w_out: bfloat16 [2, 2048, 1024], P('pp', 'fsdp'), may hold values from -0.5 to 0.5
Outputs:
- section_out: bfloat16 [2, 2, 2048, 2048], P('pp', None, 'fsdp')
- grad_qkv: float32 [2, 2048, 1536], P('pp', 'fsdp')
- grad_out: float32 [2, 2048, 1024], P('pp', 'fsdp')
- grad_gain: float32 [2, 2048], P('pp', 'fsdp')
The draws below stay inside these ranges and needn't reach their ends.
All inputs are finite; a program needn't handle non-finite values.
Results may differ from the reference program's by a relative error of at most 0.02.
Values may be sent and summed in bfloat16 or wider, within the bound.
A program may use at most 128 MiB of HBM per device.

```python
import jax
import jax.numpy as jnp
from jax import lax

D = 2048
HEADS = 16
KV_HEADS = 4
HEAD_DIM = 64
SEQ = 128
MB = 2
LAYERS = 2
TOKENS = 2048
INNER = 1024
QKV = 1536
N_FSDP = 16


def raised(drawn, rng, source, target, blocks, factor):
    def block_of(dim):
        return (jnp.arange(drawn.shape[dim]) // (drawn.shape[dim] // blocks)).reshape((-1,) + (1,) * (drawn.ndim - 1 - dim))

    first = jax.random.permutation(rng, blocks)[block_of(target)]
    far = (block_of(target) + blocks // 2) % blocks
    return jnp.where((block_of(source) == first) | (block_of(source) == far), factor * drawn, drawn)


def levels(key, shape, shards, smallest, high):
    def one(dim, shards_of):
        steps = jax.random.uniform(jax.random.fold_in(jax.random.fold_in(key, 6), dim), (shards_of,), jnp.float32, smallest / len(shards), high / len(shards))
        return jnp.repeat(jnp.exp(steps), shape[dim] // shards_of).reshape((-1,) + (1,) * (len(shape) - dim - 1))

    level = one(*shards[0])
    for cut in shards[1:]:
        level = level * one(*cut)
    return level


def gaussian(key, dims, scale, reach, cuts=(), kind=jnp.bfloat16):
    entries = jax.random.normal(key, dims, jnp.float32) * scale
    if len(cuts) > 0:
        entries = levels(key, dims, cuts, -0.22, 0.18) * entries
    return jnp.clip(entries, min=-reach, max=reach).astype(kind)


def noise_with(rng, dims, width, bound, pieces, heavy, kind=jnp.bfloat16):
    values = width * jax.random.normal(rng, dims, jnp.float32)
    if pieces:
        values = values * levels(rng, dims, pieces, -0.22, 0.18)
    return jnp.clip(raised(values, jax.random.fold_in(rng, 3), *heavy), -bound, bound).astype(kind)


def setup_inputs(seed: int = 0) -> dict:
    key_list = jax.random.split(jax.random.key(seed), 6)
    inputs = gaussian(key_list[0], (MB, TOKENS, D), 1.0, 6.0, ((1, 16),))
    cotangent = noise_with(key_list[1], (MB, TOKENS, D), ((MB * TOKENS) ** -0.5), 0.125, ((1, 16),), (1, 2, 16, 2.0))
    gains = jnp.clip(1.0 + 0.1 * jax.random.normal(key_list[2], (LAYERS, D), jnp.float32), 0.5, 1.5).astype(jnp.bfloat16)
    w_qkv = gaussian(key_list[3], (LAYERS, D, QKV), D ** -0.5, 0.125, ((0, 2), (1, 16)))
    w_out = gaussian(key_list[4], (LAYERS, D, INNER), (INNER // 8) ** -0.5, 0.5, ((0, 2), (1, 16)))
    return {"inputs": inputs, "cotangent": cotangent, "gains": gains, "w_qkv": w_qkv, "w_out": w_out}


def mix(form, left, right):
    return jnp.einsum(form, left.astype(jnp.float32), right.astype(jnp.float32))

def rope_tables(length):
    positions = jnp.arange(length, dtype=jnp.float32)
    freqs = 500000.0 ** (-jnp.arange(HEAD_DIM // 2, dtype=jnp.float32) * 2.0 / HEAD_DIM)
    angles = positions[:, None] * freqs[None, :]
    cosine = jnp.concatenate([jnp.cos(angles), jnp.cos(angles)], axis=1)
    sine = jnp.concatenate([jnp.sin(angles), jnp.sin(angles)], axis=1)
    return (cosine, sine)

def rotate_half(values):
    first = values[..., :HEAD_DIM // 2]
    second = values[..., HEAD_DIM // 2:]
    return jnp.concatenate([-second, first], axis=-1)

def apply_rope(values, cosine, sine):
    return values * cosine[:, None, :] + rotate_half(values) * sine[:, None, :]

def undo_rope(grads, cosine, sine):
    return grads * cosine[:, None, :] - rotate_half(grads * sine[:, None, :])

def layer_forward(layer_in, gain, w_qkv, w_out, cosine, sine):
    length = layer_in.shape[0]
    group = HEADS // KV_HEADS
    inner = HEADS * HEAD_DIM
    kv_width = KV_HEADS * HEAD_DIM
    values = layer_in.astype(jnp.float32)
    scale_inv = lax.rsqrt(lax.optimization_barrier(jnp.mean(values * values, axis=-1, keepdims=True)) + 1e-05)
    normed = (values * scale_inv * gain.astype(jnp.float32)).astype(jnp.bfloat16)
    joined = jnp.dot(normed, w_qkv, preferred_element_type=jnp.float32)
    queries = apply_rope(joined[:, :inner].reshape(length, HEADS, HEAD_DIM), cosine, sine).astype(jnp.bfloat16)
    keys = apply_rope(joined[:, inner:inner + kv_width].reshape(length, KV_HEADS, HEAD_DIM), cosine, sine).astype(jnp.bfloat16)
    values_v = joined[:, inner + kv_width:].reshape(length, KV_HEADS, HEAD_DIM).astype(jnp.bfloat16)
    grouped = queries.reshape(length, KV_HEADS, group, HEAD_DIM)
    scores = mix('skgh,tkh->kgst', grouped, keys) * HEAD_DIM ** (-0.5)
    causal = jnp.arange(length)[:, None] >= jnp.arange(length)[None, :]
    weights = jnp.where(causal, jnp.exp(scores), 0.0)
    probs = (weights / lax.optimization_barrier(jnp.sum(weights, axis=-1, keepdims=True))).astype(jnp.bfloat16)
    context = mix('kgst,tkh->skgh', probs, values_v).reshape(length, inner).astype(jnp.bfloat16)
    mixed = values + jnp.dot(context, w_out.T, preferred_element_type=jnp.float32)
    saved = (values, scale_inv, normed, grouped, keys, values_v, probs, context)
    return (mixed.astype(jnp.bfloat16), saved)

def layer_backward(grad_in, saved, gain, w_qkv, w_out, cosine, sine):
    values, scale_inv, normed, grouped, keys, values_v, probs, context = saved
    length = grad_in.shape[0]
    group = HEADS // KV_HEADS
    inner = HEADS * HEAD_DIM
    kv_width = KV_HEADS * HEAD_DIM
    grad_ctx = jnp.dot(grad_in, w_out, preferred_element_type=jnp.float32).astype(jnp.bfloat16)
    grad_ctx = grad_ctx.reshape(length, KV_HEADS, group, HEAD_DIM)
    grad_probs = mix('skgh,tkh->kgst', grad_ctx, values_v)
    grad_values = mix('kgst,skgh->tkh', probs, grad_ctx)
    probs_wide = probs.astype(jnp.float32)
    grad_scores = probs_wide * (grad_probs - lax.optimization_barrier(jnp.sum(grad_probs * probs_wide, axis=-1, keepdims=True)))
    grad_scores = (grad_scores * HEAD_DIM ** (-0.5)).astype(jnp.bfloat16)
    grad_queries = mix('kgst,tkh->skgh', grad_scores, keys).reshape(length, HEADS, HEAD_DIM)
    grad_keys = mix('kgst,skgh->tkh', grad_scores, grouped)
    grad_joined = jnp.concatenate([undo_rope(grad_queries, cosine, sine).reshape(length, inner), undo_rope(grad_keys, cosine, sine).reshape(length, kv_width), grad_values.reshape(length, kv_width)], axis=1).astype(jnp.bfloat16)
    grad_normed = jnp.dot(grad_joined, w_qkv.T, preferred_element_type=jnp.float32)
    scaled = grad_normed * gain.astype(jnp.float32)
    grad_x = scale_inv * scaled - values * scale_inv ** 3 * lax.optimization_barrier(jnp.mean(scaled * values, axis=-1, keepdims=True))
    grad_x = grad_x + grad_in.astype(jnp.float32)
    return (grad_x.astype(jnp.bfloat16), grad_joined)

def reference(inputs, cotangent, gains, w_qkv, w_out):
    cosine, sine = rope_tables(SEQ)
    forward_many = jax.vmap(layer_forward, in_axes=(0, None, None, None, None, None))
    backward_many = jax.vmap(layer_backward, in_axes=(0, 0, None, None, None, None, None))
    activations = inputs.reshape(MB * N_FSDP, SEQ, D)
    layer_inputs = []
    outputs = []
    for section_number in range(LAYERS):
        layer_inputs.append(activations)
        activations = forward_many(activations, gains[section_number], w_qkv[section_number], w_out[section_number], cosine, sine)[0]
        outputs.append(activations.reshape(MB, TOKENS, D))

    def split_rows(array):
        return jnp.swapaxes(array.reshape(MB, N_FSDP, SEQ, array.shape[-1]), 0, 1)

    def add_device(total, items):
        part_normed, part_joined, part_grad, part_context = items
        term = jnp.concatenate([mix('msd,msj->dj', part_normed, part_joined), mix('msd,msj->dj', part_grad, part_context)], axis=1)
        rounded = lax.optimization_barrier(term.astype(jnp.bfloat16))
        return (total + rounded.astype(jnp.float32), None)
    grads = cotangent.reshape(MB * N_FSDP, SEQ, D)
    grads_qkv = []
    grads_out = []
    grads_gain = []
    for section_number in reversed(range(LAYERS)):
        saved = forward_many(layer_inputs[section_number], gains[section_number], w_qkv[section_number], w_out[section_number], cosine, sine)[1]
        grad_x, grad_joined = backward_many(grads, saved, gains[section_number], w_qkv[section_number], w_out[section_number], cosine, sine)
        total = lax.scan(add_device, jnp.zeros((D, QKV + INNER), jnp.float32), (split_rows(saved[2]), split_rows(grad_joined), split_rows(grads), split_rows(saved[7])))[0]
        part_qkv = total[:, :QKV]
        grads_qkv.append(part_qkv)
        grads_out.append(total[:, QKV:])
        grads_gain.append(lax.optimization_barrier(jnp.sum(part_qkv * w_qkv[section_number].astype(jnp.float32), axis=1)) / gains[section_number].astype(jnp.float32))
        grads = grad_x
    return (jnp.stack(outputs), jnp.stack(grads_qkv[::-1]), jnp.stack(grads_out[::-1]), jnp.stack(grads_gain[::-1]))
```

```python
import jax
import jax.numpy as jnp
from jax import lax
from jax.sharding import PartitionSpec as P

HEADS = 16
KV_HEADS = 4
HEAD_DIM = 64


def shifted(value, axis, steps):
    count = lax.axis_size(axis)
    leading, last = (max(0, -steps), min(count, count - steps))
    return lax.ppermute(value, axis, [(source, source + steps) for source in range(leading, last)])


def mix(form, left, right):
    return jnp.einsum(form, left, right, preferred_element_type=jnp.float32)


def rope_tables(length):
    positions = jnp.arange(length, dtype=jnp.float32)
    freqs = 500000.0 ** (-jnp.arange(HEAD_DIM // 2, dtype=jnp.float32) * 2.0 / HEAD_DIM)
    angles = positions[:, None] * freqs[None, :]
    cosine = jnp.concatenate([jnp.cos(angles), jnp.cos(angles)], axis=1)
    sine = jnp.concatenate([jnp.sin(angles), jnp.sin(angles)], axis=1)
    return (cosine, sine)


def rotate_half(values):
    first = values[..., : HEAD_DIM // 2]
    second = values[..., HEAD_DIM // 2 :]
    return jnp.concatenate([-second, first], axis=-1)


def apply_rope(values, cosine, sine):
    return values * cosine[:, None, :] + rotate_half(values) * sine[:, None, :]


def undo_rope(grads, cosine, sine):
    return grads * cosine[:, None, :] - rotate_half(grads * sine[:, None, :])


def layer_forward(layer_in, gain, w_qkv, w_out, cosine, sine):
    length = layer_in.shape[0]
    group = HEADS // KV_HEADS
    inner = HEADS * HEAD_DIM
    kv_width = KV_HEADS * HEAD_DIM
    values = layer_in.astype(jnp.float32)
    scale_inv = lax.rsqrt(jnp.mean(values * values, axis=-1, keepdims=True) + 1e-05)
    normed = (values * scale_inv * gain.astype(jnp.float32)).astype(jnp.bfloat16)
    joined = jnp.dot(normed, w_qkv, preferred_element_type=jnp.float32)
    queries = apply_rope(joined[:, :inner].reshape(length, HEADS, HEAD_DIM), cosine, sine).astype(
        jnp.bfloat16
    )
    keys = apply_rope(
        joined[:, inner : inner + kv_width].reshape(length, KV_HEADS, HEAD_DIM), cosine, sine
    ).astype(jnp.bfloat16)
    values_v = (
        joined[:, inner + kv_width :].reshape(length, KV_HEADS, HEAD_DIM).astype(jnp.bfloat16)
    )
    grouped = queries.reshape(length, KV_HEADS, group, HEAD_DIM)
    scores = mix("skgh,tkh->kgst", grouped, keys) * HEAD_DIM ** (-0.5)
    causal = jnp.arange(length)[:, None] >= jnp.arange(length)[None, :]
    weights = jnp.where(causal, jnp.exp(scores), 0.0)
    probs = (weights / jnp.sum(weights, axis=-1, keepdims=True)).astype(jnp.bfloat16)
    context = mix("kgst,tkh->skgh", probs, values_v).reshape(length, inner).astype(jnp.bfloat16)
    mixed = values + mix("sc,dc->sd", context, w_out)
    saved = (values, scale_inv, normed, grouped, keys, values_v, probs, context)
    return (mixed.astype(jnp.bfloat16), saved)


def layer_backward(grad_in, saved, gain, w_qkv, w_out, cosine, sine):
    values, scale_inv, normed, grouped, keys, values_v, probs, context = saved
    length = grad_in.shape[0]
    group = HEADS // KV_HEADS
    inner = HEADS * HEAD_DIM
    kv_width = KV_HEADS * HEAD_DIM
    grad_ctx = jnp.dot(grad_in, w_out, preferred_element_type=jnp.float32).astype(jnp.bfloat16)
    grad_ctx = grad_ctx.reshape(length, KV_HEADS, group, HEAD_DIM)
    grad_probs = mix("skgh,tkh->kgst", grad_ctx, values_v)
    grad_values = mix("kgst,skgh->tkh", probs, grad_ctx)
    probs_wide = probs.astype(jnp.float32)
    grad_scores = probs_wide * (
        grad_probs - jnp.sum(grad_probs * probs_wide, axis=-1, keepdims=True)
    )
    grad_scores = (grad_scores * HEAD_DIM ** (-0.5)).astype(jnp.bfloat16)
    grad_queries = mix("kgst,tkh->skgh", grad_scores, keys).reshape(length, HEADS, HEAD_DIM)
    grad_keys = mix("kgst,skgh->tkh", grad_scores, grouped)
    grad_joined = jnp.concatenate(
        [
            undo_rope(grad_queries, cosine, sine).reshape(length, inner),
            undo_rope(grad_keys, cosine, sine).reshape(length, kv_width),
            grad_values.reshape(length, kv_width),
        ],
        axis=1,
    ).astype(jnp.bfloat16)
    grad_normed = mix("sj,dj->sd", grad_joined, w_qkv)
    scaled = grad_normed * gain.astype(jnp.float32)
    grad_x = scale_inv * scaled - values * scale_inv**3 * jnp.mean(
        scaled * values, axis=-1, keepdims=True
    )
    grad_x = grad_x + grad_in.astype(jnp.float32)
    return (grad_x.astype(jnp.bfloat16), grad_joined)


def staged(inputs, cotangent, gains, w_qkv, w_out):
    section_count = lax.axis_size("pp")
    section_index = lax.axis_index("pp")
    full_qkv, full_out, full_gain = (
        lax.all_gather(w_qkv[0], "fsdp", axis=0, tiled=True),
        lax.all_gather(w_out[0], "fsdp", axis=0, tiled=True),
        lax.all_gather(gains[0], "fsdp", axis=0, tiled=True),
    )
    micro_count, length, width = inputs.shape
    joined_width = full_qkv.shape[1]
    inner = full_out.shape[1]
    tick_count = micro_count + section_count - 1
    last_section = section_count - 1
    cosine, sine = rope_tables(length)

    def forward_tick(carry, tick):
        received, saved_in, outputs = carry
        slot = tick - section_index
        valid = jnp.logical_and(slot >= 0, slot < micro_count)
        slot_index = jnp.clip(slot, 0, micro_count - 1)
        first_in = lax.dynamic_index_in_dim(inputs, slot_index, 0, keepdims=False)
        layer_in = jnp.where(section_index == 0, first_in, received)

        def forward_run_layer(operands):
            current, kept_in, kept_out = operands
            layer_out = layer_forward(current, full_gain, full_qkv, full_out, cosine, sine)[0]
            kept_in = lax.dynamic_update_index_in_dim(kept_in, current, slot_index, 0)
            kept_out = lax.dynamic_update_index_in_dim(kept_out, layer_out, slot_index, 0)
            return (layer_out, kept_in, kept_out)

        def forward_skip_layer(operands):
            current, kept_in, kept_out = operands
            return (jnp.zeros_like(current), kept_in, kept_out)

        layer_out, saved_in, outputs = lax.cond(
            valid, forward_run_layer, forward_skip_layer, (layer_in, saved_in, outputs)
        )
        received = shifted(layer_out, "pp", 1)
        return ((received, saved_in, outputs), None)

    blank = jnp.zeros((micro_count, length, width), jnp.bfloat16)
    start_carry = (jnp.zeros((length, width), jnp.bfloat16), blank, blank)
    (_, saved_in, outputs), _ = lax.scan(forward_tick, start_carry, jnp.arange(tick_count))
    extra = (
        blank,
        jnp.zeros((micro_count, length, inner), jnp.bfloat16),
        jnp.zeros((micro_count, length, joined_width), jnp.bfloat16),
        blank,
    )

    def backward_tick(carry, tick):
        received, kept = carry
        slot = tick - (last_section - section_index)
        valid = jnp.logical_and(slot >= 0, slot < micro_count)
        slot_index = jnp.clip(slot, 0, micro_count - 1)
        last_in = lax.dynamic_index_in_dim(cotangent, slot_index, 0, keepdims=False)
        grad_in = jnp.where(section_index == last_section, last_in, received)

        def backward_run_layer(operands):
            current, store = operands
            layer_in = lax.dynamic_index_in_dim(saved_in, slot_index, 0, keepdims=False)
            saved = layer_forward(layer_in, full_gain, full_qkv, full_out, cosine, sine)[1]
            grad_x, grad_joined = layer_backward(
                current, saved, full_gain, full_qkv, full_out, cosine, sine
            )
            pieces = (saved[2], saved[7], grad_joined, current)
            store = tuple(
                (
                    lax.dynamic_update_index_in_dim(buffer, piece, slot_index, 0)
                    for buffer, piece in zip(store, pieces)
                )
            )
            return (grad_x, store)

        def backward_skip_layer(operands):
            current, store = operands
            return (jnp.zeros_like(current), store)

        grad_x, kept = lax.cond(valid, backward_run_layer, backward_skip_layer, (grad_in, kept))
        received = shifted(grad_x, "pp", -1)
        return ((received, kept), None)

    (_, extra), _ = lax.scan(
        backward_tick, (jnp.zeros((length, width), jnp.bfloat16), extra), jnp.arange(tick_count)
    )
    normed_all, context_all, joined_all, incoming_all = extra
    summed = lax.psum_scatter(
        jnp.concatenate(
            [
                mix("msd,msj->dj", normed_all, joined_all),
                mix("msd,msc->dc", incoming_all, context_all),
            ],
            axis=1,
        ).astype(jnp.bfloat16),
        "fsdp",
        scatter_dimension=0,
        tiled=True,
    ).astype(jnp.float32)
    grad_qkv = summed[:, :joined_width]
    grad_out = summed[:, joined_width:]
    grad_gain = jnp.sum(grad_qkv * w_qkv[0].astype(jnp.float32), axis=1) / gains[0].astype(
        jnp.float32
    )
    return (outputs[None], grad_qkv[None], grad_out[None], grad_gain[None])


def pick(first, own, other):
    return jax.tree.map(lambda left, right: jnp.where(first, left, right), own, other)


def two_sections(inputs, cotangent, gains, w_qkv, w_out):
    first = lax.axis_index("pp") == 0
    full_gain = lax.all_gather(gains[0], "fsdp", axis=0, tiled=True)
    full_qkv = lax.all_gather(w_qkv[0], "fsdp", axis=0, tiled=True)
    full_out = lax.all_gather(w_out[0], "fsdp", axis=0, tiled=True)
    micro_count, length, width = inputs.shape
    cosine, sine = rope_tables(length)
    weights = (full_gain, full_qkv, full_out, cosine, sine)
    early, sent = [], []
    for micro in range(micro_count):
        out, saved = layer_forward(inputs[micro], *weights)
        early.append((out, saved))
        sent.append(shifted(out, "pp", 1))
    late, back = [], []
    for micro in range(micro_count):
        out, saved = layer_forward(sent[micro], *weights)
        grad_x = layer_backward(cotangent[micro], saved, *weights)[0]
        late.append((out, saved))
        back.append(shifted(grad_x, "pp", -1))
    kept = []
    for micro in range(micro_count):
        out, saved = pick(first, early[micro], late[micro])
        grad_in = jnp.where(first, back[micro], cotangent[micro])
        grad_joined = layer_backward(grad_in, saved, *weights)[1]
        kept.append((out, saved[2], grad_joined, grad_in, saved[7]))
    outputs, normed, joined, incoming, context = (jnp.stack(piece) for piece in zip(*kept))
    return finish(outputs, normed, joined, incoming, context, gains, w_qkv)


def finish(outputs, normed, joined, incoming, context, gains, w_qkv):
    joined_width = joined.shape[-1]
    summed = lax.psum_scatter(
        jnp.concatenate(
            [mix("msd,msj->dj", normed, joined), mix("msd,msc->dc", incoming, context)], axis=1
        ).astype(jnp.bfloat16),
        "fsdp",
        scatter_dimension=0,
        tiled=True,
    ).astype(jnp.float32)
    grad_qkv = summed[:, :joined_width]
    grad_out = summed[:, joined_width:]
    grad_gain = jnp.sum(grad_qkv * w_qkv[0].astype(jnp.float32), axis=1) / gains[0].astype(
        jnp.float32
    )
    return (outputs[None], grad_qkv[None], grad_out[None], grad_gain[None])


def solution(mesh):
    return jax.shard_map(
        two_sections if mesh.shape["pp"] == 2 else staged,
        mesh=mesh,
        in_specs=(
            P(None, "fsdp", None),
            P(None, "fsdp", None),
            P("pp", "fsdp"),
            P("pp", "fsdp", None),
            P("pp", "fsdp", None),
        ),
        out_specs=(
            P("pp", None, "fsdp", None),
            P("pp", "fsdp", None),
            P("pp", "fsdp", None),
            P("pp", "fsdp"),
        ),
        check_vma=False,
    )
```

```python
import functools

import jax
import jax.numpy as jnp
from jax import lax
from jax.experimental import pallas as pl
from jax.experimental.pallas import tpu as pltpu
from jax.sharding import PartitionSpec as P

HEADS = 16
KV_HEADS = 4
HEAD_DIM = 64
MESH = pl.DeviceIdType.MESH


def shifted(value, axis, steps):
    count = lax.axis_size(axis)
    leading, last = (max(0, -steps), min(count, count - steps))
    return lax.ppermute(value, axis, [(source, source + steps) for source in range(leading, last)])


def mix(form, left, right):
    return jnp.einsum(form, left, right, preferred_element_type=jnp.float32)


def rope_tables(length):
    positions = jnp.arange(length, dtype=jnp.float32)
    freqs = 500000.0 ** (-jnp.arange(HEAD_DIM // 2, dtype=jnp.float32) * 2.0 / HEAD_DIM)
    angles = positions[:, None] * freqs[None, :]
    cosine = jnp.concatenate([jnp.cos(angles), jnp.cos(angles)], axis=1)
    sine = jnp.concatenate([jnp.sin(angles), jnp.sin(angles)], axis=1)
    return (cosine, sine)


def rotate_half(values):
    first = values[..., : HEAD_DIM // 2]
    second = values[..., HEAD_DIM // 2 :]
    return jnp.concatenate([-second, first], axis=-1)


def apply_rope(values, cosine, sine):
    return values * cosine[:, None, :] + rotate_half(values) * sine[:, None, :]


def undo_rope(grads, cosine, sine):
    return grads * cosine[:, None, :] - rotate_half(grads * sine[:, None, :])


def layer_forward(layer_in, gain, w_qkv, w_out, cosine, sine):
    length = layer_in.shape[0]
    group = HEADS // KV_HEADS
    inner = HEADS * HEAD_DIM
    kv_width = KV_HEADS * HEAD_DIM
    values = layer_in.astype(jnp.float32)
    scale_inv = lax.rsqrt(jnp.mean(values * values, axis=-1, keepdims=True) + 1e-05)
    normed = (values * scale_inv * gain.astype(jnp.float32)).astype(jnp.bfloat16)
    joined = jnp.dot(normed, w_qkv, preferred_element_type=jnp.float32)
    queries = apply_rope(joined[:, :inner].reshape(length, HEADS, HEAD_DIM), cosine, sine).astype(
        jnp.bfloat16
    )
    keys = apply_rope(
        joined[:, inner : inner + kv_width].reshape(length, KV_HEADS, HEAD_DIM), cosine, sine
    ).astype(jnp.bfloat16)
    values_v = (
        joined[:, inner + kv_width :].reshape(length, KV_HEADS, HEAD_DIM).astype(jnp.bfloat16)
    )
    grouped = queries.reshape(length, KV_HEADS, group, HEAD_DIM)
    scores = mix("skgh,tkh->kgst", grouped, keys) * HEAD_DIM ** (-0.5)
    causal = jnp.arange(length)[:, None] >= jnp.arange(length)[None, :]
    weights = jnp.where(causal, jnp.exp(scores), 0.0)
    probs = (weights / jnp.sum(weights, axis=-1, keepdims=True)).astype(jnp.bfloat16)
    context = mix("kgst,tkh->skgh", probs, values_v).reshape(length, inner).astype(jnp.bfloat16)
    mixed = values + mix("sc,dc->sd", context, w_out)
    saved = (values, scale_inv, normed, grouped, keys, values_v, probs, context)
    return (mixed.astype(jnp.bfloat16), saved)


def layer_backward(grad_in, saved, gain, w_qkv, w_out, cosine, sine):
    values, scale_inv, normed, grouped, keys, values_v, probs, context = saved
    length = grad_in.shape[0]
    group = HEADS // KV_HEADS
    inner = HEADS * HEAD_DIM
    kv_width = KV_HEADS * HEAD_DIM
    grad_ctx = jnp.dot(grad_in, w_out, preferred_element_type=jnp.float32).astype(jnp.bfloat16)
    grad_ctx = grad_ctx.reshape(length, KV_HEADS, group, HEAD_DIM)
    grad_probs = mix("skgh,tkh->kgst", grad_ctx, values_v)
    grad_values = mix("kgst,skgh->tkh", probs, grad_ctx)
    probs_wide = probs.astype(jnp.float32)
    grad_scores = probs_wide * (
        grad_probs - jnp.sum(grad_probs * probs_wide, axis=-1, keepdims=True)
    )
    grad_scores = (grad_scores * HEAD_DIM ** (-0.5)).astype(jnp.bfloat16)
    grad_queries = mix("kgst,tkh->skgh", grad_scores, keys).reshape(length, HEADS, HEAD_DIM)
    grad_keys = mix("kgst,skgh->tkh", grad_scores, grouped)
    grad_joined = jnp.concatenate(
        [
            undo_rope(grad_queries, cosine, sine).reshape(length, inner),
            undo_rope(grad_keys, cosine, sine).reshape(length, kv_width),
            grad_values.reshape(length, kv_width),
        ],
        axis=1,
    ).astype(jnp.bfloat16)
    grad_normed = mix("sj,dj->sd", grad_joined, w_qkv)
    scaled = grad_normed * gain.astype(jnp.float32)
    grad_x = scale_inv * scaled - values * scale_inv**3 * jnp.mean(
        scaled * values, axis=-1, keepdims=True
    )
    grad_x = grad_x + grad_in.astype(jnp.float32)
    return (grad_x.astype(jnp.bfloat16), grad_joined)


def staged(inputs, cotangent, gains, w_qkv, w_out):
    section_count = lax.axis_size("pp")
    section_index = lax.axis_index("pp")
    full_qkv, full_out, full_gain = (
        lax.all_gather(w_qkv[0], "fsdp", axis=0, tiled=True),
        lax.all_gather(w_out[0], "fsdp", axis=0, tiled=True),
        lax.all_gather(gains[0], "fsdp", axis=0, tiled=True),
    )
    micro_count, length, width = inputs.shape
    joined_width = full_qkv.shape[1]
    inner = full_out.shape[1]
    tick_count = micro_count + section_count - 1
    last_section = section_count - 1
    cosine, sine = rope_tables(length)

    def forward_tick(carry, tick):
        received, saved_in, outputs = carry
        slot = tick - section_index
        valid = jnp.logical_and(slot >= 0, slot < micro_count)
        slot_index = jnp.clip(slot, 0, micro_count - 1)
        first_in = lax.dynamic_index_in_dim(inputs, slot_index, 0, keepdims=False)
        layer_in = jnp.where(section_index == 0, first_in, received)

        def forward_run_layer(operands):
            current, kept_in, kept_out = operands
            layer_out = layer_forward(current, full_gain, full_qkv, full_out, cosine, sine)[0]
            kept_in = lax.dynamic_update_index_in_dim(kept_in, current, slot_index, 0)
            kept_out = lax.dynamic_update_index_in_dim(kept_out, layer_out, slot_index, 0)
            return (layer_out, kept_in, kept_out)

        def forward_skip_layer(operands):
            current, kept_in, kept_out = operands
            return (jnp.zeros_like(current), kept_in, kept_out)

        layer_out, saved_in, outputs = lax.cond(
            valid, forward_run_layer, forward_skip_layer, (layer_in, saved_in, outputs)
        )
        received = shifted(layer_out, "pp", 1)
        return ((received, saved_in, outputs), None)

    blank = jnp.zeros((micro_count, length, width), jnp.bfloat16)
    start_carry = (jnp.zeros((length, width), jnp.bfloat16), blank, blank)
    (_, saved_in, outputs), _ = lax.scan(forward_tick, start_carry, jnp.arange(tick_count))
    extra = (
        blank,
        jnp.zeros((micro_count, length, inner), jnp.bfloat16),
        jnp.zeros((micro_count, length, joined_width), jnp.bfloat16),
        blank,
    )

    def backward_tick(carry, tick):
        received, kept = carry
        slot = tick - (last_section - section_index)
        valid = jnp.logical_and(slot >= 0, slot < micro_count)
        slot_index = jnp.clip(slot, 0, micro_count - 1)
        last_in = lax.dynamic_index_in_dim(cotangent, slot_index, 0, keepdims=False)
        grad_in = jnp.where(section_index == last_section, last_in, received)

        def backward_run_layer(operands):
            current, store = operands
            layer_in = lax.dynamic_index_in_dim(saved_in, slot_index, 0, keepdims=False)
            saved = layer_forward(layer_in, full_gain, full_qkv, full_out, cosine, sine)[1]
            grad_x, grad_joined = layer_backward(
                current, saved, full_gain, full_qkv, full_out, cosine, sine
            )
            pieces = (saved[2], saved[7], grad_joined, current)
            store = tuple(
                (
                    lax.dynamic_update_index_in_dim(buffer, piece, slot_index, 0)
                    for buffer, piece in zip(store, pieces)
                )
            )
            return (grad_x, store)

        def backward_skip_layer(operands):
            current, store = operands
            return (jnp.zeros_like(current), store)

        grad_x, kept = lax.cond(valid, backward_run_layer, backward_skip_layer, (grad_in, kept))
        received = shifted(grad_x, "pp", -1)
        return ((received, kept), None)

    (_, extra), _ = lax.scan(
        backward_tick, (jnp.zeros((length, width), jnp.bfloat16), extra), jnp.arange(tick_count)
    )
    normed_all, context_all, joined_all, incoming_all = extra
    summed = lax.psum_scatter(
        jnp.concatenate(
            [
                mix("msd,msj->dj", normed_all, joined_all),
                mix("msd,msc->dc", incoming_all, context_all),
            ],
            axis=1,
        ).astype(jnp.bfloat16),
        "fsdp",
        scatter_dimension=0,
        tiled=True,
    ).astype(jnp.float32)
    grad_qkv = summed[:, :joined_width]
    grad_out = summed[:, joined_width:]
    grad_gain = jnp.sum(grad_qkv * w_qkv[0].astype(jnp.float32), axis=1) / gains[0].astype(
        jnp.float32
    )
    return (outputs[None], grad_qkv[None], grad_out[None], grad_gain[None])


def place(count):
    me = lax.axis_index("fsdp")
    return (count // 4, me // 4, (me // 2) % 2, me % 2)


def at(outer, side, core):
    return (outer * 2 + side) * 2 + core


def remote(source, target, send_sem, recv_sem, device):
    return pltpu.make_async_remote_copy(
        src_ref=source,
        dst_ref=target,
        send_sem=send_sem,
        recv_sem=recv_sem,
        device_id={"fsdp": device},
        device_id_type=MESH,
    )


def greet(outers, outer, side, core):
    barrier = pltpu.get_barrier_semaphore()
    peers = [at((outer + step) % outers, side, core) for step in range(1, outers)]
    peers += [at(outer, 1 - side, core), at(outer, side, 1 - core)]
    for peer in peers:
        pl.semaphore_signal(barrier, inc=1, device_id={"fsdp": peer}, device_id_type=MESH)
    pl.semaphore_wait(barrier, len(peers))


def gather_kernel(
    count, qkv, out, gain, full_qkv, full_out, full_gain, own, z_out, z_in, x_out, x_in, c_out, c_in
):
    outers, outer, side, core = place(count)
    greet(outers, outer, side, core)
    parts = [(gain, full_gain, 0, gain.shape[0])]
    for source, target in ((qkv, full_qkv), (out, full_out)):
        half = source.shape[0] // 2
        parts += [(source, target, 0, half), (source, target, half, half)]
    beside, partner = at(outer, 1 - side, core), at(outer, side, 1 - core)

    def rows(part, owner):
        source, target, start, size = part
        first = pl.multiple_of(owner * source.shape[0] + start, 16)
        return target.at[pl.ds(first, size)]

    started, local = [], []

    def send(source, target, send_sem, recv_sem, device):
        copy = remote(source, target, send_sem, recv_sem, device)
        copy.start()
        started.append(copy)

    for j, part in enumerate(parts):
        source, target, start, size = part
        block, spot = source.at[pl.ds(start, size)], rows(part, at(outer, side, core))
        for step in range(1, outers):
            peer = at((outer + step) % outers, side, core)
            send(block, spot, z_out.at[step, j], z_in.at[step, j], peer)
        send(block, spot, x_out.at[0, j], x_in.at[0, j], beside)
        send(block, spot, c_out.at[0, 0, j], c_in.at[0, 0, j], partner)
        copy = pltpu.make_async_copy(block, spot, own.at[j])
        copy.start()
        local.append(copy)
    for j, part in enumerate(parts):
        for step in range(1, outers):
            spot = rows(part, at((outer + outers - step) % outers, side, core))
            remote(spot, spot, z_out.at[step, j], z_in.at[step, j], beside).wait_recv()
            send(spot, spot, x_out.at[step, j], x_in.at[step, j], beside)
            send(spot, spot, c_out.at[0, step, j], c_in.at[0, step, j], partner)
        for step in range(outers):
            spot = rows(part, at((outer + outers - step) % outers, 1 - side, core))
            remote(spot, spot, x_out.at[step, j], x_in.at[step, j], beside).wait_recv()
            send(spot, spot, c_out.at[1, step, j], c_in.at[1, step, j], partner)
    for j, part in enumerate(parts):
        for over in range(2):
            for step in range(outers):
                origin = at(
                    (outer + outers - step) % outers, 1 - side if over else side, 1 - core
                )
                spot = rows(part, origin)
                remote(
                    spot, spot, c_out.at[over, step, j], c_in.at[over, step, j], partner
                ).wait_recv()
    for copy in started:
        copy.wait_send()
    for copy in local:
        copy.wait()


def gather(qkv, out, gain):
    count = lax.axis_size("fsdp")
    outers = count // 4
    gain = jnp.broadcast_to(gain[None], (16, gain.shape[0]))
    sems = [(outers, 5), (outers, 5), (outers, 5), (outers, 5), (2, outers, 5), (2, outers, 5)]
    full_qkv, full_out, full_gain = pl.pallas_call(
        functools.partial(gather_kernel, count),
        out_shape=[
            jax.ShapeDtypeStruct((count * block.shape[0], block.shape[1]), block.dtype)
            for block in (qkv, out, gain)
        ],
        in_specs=[pl.BlockSpec(memory_space=pl.ANY)] * 3,
        out_specs=[pl.BlockSpec(memory_space=pl.ANY)] * 3,
        scratch_shapes=[pltpu.SemaphoreType.DMA((5,))]
        + [pltpu.SemaphoreType.DMA(shape) for shape in sems],
        compiler_params=pltpu.CompilerParams(collective_id=0, has_side_effects=True),
    )(qkv, out, gain)
    return (full_qkv, full_out, full_gain.reshape(count, 16, -1)[:, 0].reshape(-1))


def reduce_kernel(
    count, normed, joined, incoming, context, sum_qkv, sum_out,
    c_buf, own, c_got, x_buf, x_got, z_buf, z_got, c_out, c_in, x_out, x_in, z_out, z_in,
):
    outers, outer, side, core = place(count)
    depth, width = sum_qkv.shape
    beside, partner = at(outer, 1 - side, core), at(outer, side, 1 - core)
    greet(outers, outer, side, core)

    def term(index, target):
        columns = pl.ds(pl.multiple_of(index * depth, depth), depth)
        form = (((0,), (0,)), ((), ()))
        target[:, :width] = lax.dot_general(
            normed[:, columns], joined[...], form, preferred_element_type=jnp.float32
        ).astype(jnp.bfloat16)
        target[:, width:] = lax.dot_general(
            incoming[:, columns], context[...], form, preferred_element_type=jnp.float32
        ).astype(jnp.bfloat16)

    def to_core(k):
        return remote(c_buf.at[k], c_got.at[k], c_out.at[k], c_in.at[k], partner)

    def to_side(k):
        return remote(x_buf.at[k], x_got.at[k], x_out.at[k], x_in.at[k], beside)

    def to_outer(k):
        peer = at((outer + k + 1) % outers, side, core)
        return remote(z_buf.at[k], z_got.at[k], z_out.at[k], z_in.at[k], peer)

    def wide(ref):
        return ref[...].astype(jnp.float32)

    def combine(k):
        to_core(k).wait_recv()
        both = (wide(own.at[k]) + wide(c_got.at[k])).astype(jnp.bfloat16)

        @pl.when(k < outers)
        def _():
            x_buf[k % outers] = both
            to_side(k % outers).start()

        @pl.when(k >= outers)
        def _():
            own[k] = both

    def one(k, carry):
        where = (outer + k + 1) % outers
        over = k // outers
        there = over * side + (1 - over) * (1 - side)
        term(at(where, there, 1 - core), c_buf.at[k])
        to_core(k).start()
        term(at(where, there, core), own.at[k])

        @pl.when(k > 0)
        def _():
            combine(k - 1)

        return carry

    lax.fori_loop(0, 2 * outers, one, 0)
    combine(2 * outers - 1)

    def two(k, carry):
        to_side(k).wait_recv()
        z_buf[k] = (wide(own.at[outers + k]) + wide(x_got.at[k])).astype(jnp.bfloat16)
        to_outer(k).start()
        return carry

    lax.fori_loop(0, outers - 1, two, 0)
    last = outers - 1
    to_side(last).wait_recv()
    total = wide(own.at[outers + last]) + wide(x_got.at[last])
    for k in range(last):
        to_outer(k).wait_recv()
        total += wide(z_got.at[k])
    sum_qkv[...] = total[:, :width]
    sum_out[...] = total[:, width:]

    for k in range(2 * outers):
        to_core(k).wait_send()
    for k in range(outers):
        to_side(k).wait_send()
    for k in range(last):
        to_outer(k).wait_send()


def reduce_terms(normed, joined, incoming, context):
    count = lax.axis_size("fsdp")
    outers = count // 4
    tokens, width = normed.shape
    depth = width // count
    columns = joined.shape[1] + context.shape[1]

    def slots(number):
        return pltpu.VMEM((number, depth, columns), jnp.bfloat16)

    numbers = (2 * outers, 2 * outers, 2 * outers, outers, outers, outers - 1, outers - 1)
    sems = (2 * outers, 2 * outers, outers, outers, outers - 1, outers - 1)
    return pl.pallas_call(
        functools.partial(reduce_kernel, count),
        out_shape=[
            jax.ShapeDtypeStruct((depth, piece.shape[1]), jnp.float32) for piece in (joined, context)
        ],
        in_specs=[pl.BlockSpec(memory_space=pltpu.VMEM)] * 4,
        out_specs=[pl.BlockSpec(memory_space=pltpu.VMEM)] * 2,
        scratch_shapes=[slots(number) for number in numbers]
        + [pltpu.SemaphoreType.DMA((number,)) for number in sems],
        compiler_params=pltpu.CompilerParams(
            collective_id=1, has_side_effects=True, vmem_limit_bytes=48 * 1024 * 1024
        ),
    )(normed, joined, incoming, context)


def pick(first, own, other):
    return jax.tree.map(lambda left, right: jnp.where(first, left, right), own, other)


def two_sections(inputs, cotangent, gains, w_qkv, w_out):
    first = lax.axis_index("pp") == 0
    full_qkv, full_out, full_gain = gather(w_qkv[0], w_out[0], gains[0])
    micro_count, length, width = inputs.shape
    cosine, sine = rope_tables(length)
    weights = (full_gain, full_qkv, full_out, cosine, sine)
    early, sent = [], []
    for micro in range(micro_count):
        out, saved = layer_forward(inputs[micro], *weights)
        early.append((out, saved))
        sent.append(shifted(out, "pp", 1))
    late, back = [], []
    for micro in range(micro_count):
        out, saved = layer_forward(sent[micro], *weights)
        grad_x = layer_backward(cotangent[micro], saved, *weights)[0]
        late.append((out, saved))
        back.append(shifted(grad_x, "pp", -1))
    kept = []
    for micro in range(micro_count):
        out, saved = pick(first, early[micro], late[micro])
        grad_in = jnp.where(first, back[micro], cotangent[micro])
        grad_joined = layer_backward(grad_in, saved, *weights)[1]
        kept.append((out, saved[2], grad_joined, grad_in, saved[7]))
    outputs, normed, joined, incoming, context = zip(*kept)
    return finish(outputs, normed, joined, incoming, context, gains, w_qkv)


def finish(outputs, normed, joined, incoming, context, gains, w_qkv):
    pieces = (jnp.concatenate(piece, axis=0) for piece in (normed, joined, incoming, context))
    grad_qkv, grad_out = reduce_terms(*pieces)
    grad_gain = jnp.sum(grad_qkv * w_qkv[0].astype(jnp.float32), axis=1) / gains[0].astype(
        jnp.float32
    )
    return (jnp.stack(outputs)[None], grad_qkv[None], grad_out[None], grad_gain[None])


def solution(mesh):
    return jax.shard_map(
        two_sections if mesh.shape["pp"] == 2 else staged,
        mesh=mesh,
        in_specs=(
            P(None, "fsdp", None),
            P(None, "fsdp", None),
            P("pp", "fsdp"),
            P("pp", "fsdp", None),
            P("pp", "fsdp", None),
        ),
        out_specs=(
            P("pp", None, "fsdp", None),
            P("pp", "fsdp", None),
            P("pp", "fsdp", None),
            P("pp", "fsdp"),
        ),
        check_vma=False,
    )
```

```python
import functools

import jax
import jax.numpy as jnp
from jax import lax
from jax.experimental import pallas as pl
from jax.experimental.pallas import tpu as pltpu
from jax.sharding import PartitionSpec as P

HEADS = 16
KV_HEADS = 4
HEAD_DIM = 64
MESH = pl.DeviceIdType.MESH


def shifted(value, axis, steps):
    count = lax.axis_size(axis)
    leading, last = (max(0, -steps), min(count, count - steps))
    return lax.ppermute(value, axis, [(source, source + steps) for source in range(leading, last)])


def mix(form, left, right):
    return jnp.einsum(form, left, right, preferred_element_type=jnp.float32)


def rope_tables(length):
    positions = jnp.arange(length, dtype=jnp.float32)
    freqs = 500000.0 ** (-jnp.arange(HEAD_DIM // 2, dtype=jnp.float32) * 2.0 / HEAD_DIM)
    angles = positions[:, None] * freqs[None, :]
    cosine = jnp.concatenate([jnp.cos(angles), jnp.cos(angles)], axis=1)
    sine = jnp.concatenate([jnp.sin(angles), jnp.sin(angles)], axis=1)
    return (cosine, sine)


def rotate_half(values):
    first = values[..., : HEAD_DIM // 2]
    second = values[..., HEAD_DIM // 2 :]
    return jnp.concatenate([-second, first], axis=-1)


def apply_rope(values, cosine, sine):
    return values * cosine[:, None, :] + rotate_half(values) * sine[:, None, :]


def undo_rope(grads, cosine, sine):
    return grads * cosine[:, None, :] - rotate_half(grads * sine[:, None, :])


def layer_forward(layer_in, gain, w_qkv, w_out, cosine, sine):
    length = layer_in.shape[0]
    group = HEADS // KV_HEADS
    inner = HEADS * HEAD_DIM
    kv_width = KV_HEADS * HEAD_DIM
    values = layer_in.astype(jnp.float32)
    scale_inv = lax.rsqrt(jnp.mean(values * values, axis=-1, keepdims=True) + 1e-05)
    normed = (values * scale_inv * gain.astype(jnp.float32)).astype(jnp.bfloat16)
    joined = jnp.dot(normed, w_qkv, preferred_element_type=jnp.float32)
    queries = apply_rope(joined[:, :inner].reshape(length, HEADS, HEAD_DIM), cosine, sine).astype(
        jnp.bfloat16
    )
    keys = apply_rope(
        joined[:, inner : inner + kv_width].reshape(length, KV_HEADS, HEAD_DIM), cosine, sine
    ).astype(jnp.bfloat16)
    values_v = (
        joined[:, inner + kv_width :].reshape(length, KV_HEADS, HEAD_DIM).astype(jnp.bfloat16)
    )
    grouped = queries.reshape(length, KV_HEADS, group, HEAD_DIM)
    scores = mix("skgh,tkh->kgst", grouped, keys) * HEAD_DIM ** (-0.5)
    causal = jnp.arange(length)[:, None] >= jnp.arange(length)[None, :]
    weights = jnp.where(causal, jnp.exp(scores), 0.0)
    probs = (weights / jnp.sum(weights, axis=-1, keepdims=True)).astype(jnp.bfloat16)
    context = mix("kgst,tkh->skgh", probs, values_v).reshape(length, inner).astype(jnp.bfloat16)
    mixed = values + mix("sc,dc->sd", context, w_out)
    saved = (values, scale_inv, normed, grouped, keys, values_v, probs, context)
    return (mixed.astype(jnp.bfloat16), saved)


def layer_backward(grad_in, saved, gain, w_qkv, w_out, cosine, sine):
    values, scale_inv, normed, grouped, keys, values_v, probs, context = saved
    length = grad_in.shape[0]
    group = HEADS // KV_HEADS
    inner = HEADS * HEAD_DIM
    kv_width = KV_HEADS * HEAD_DIM
    grad_ctx = jnp.dot(grad_in, w_out, preferred_element_type=jnp.float32).astype(jnp.bfloat16)
    grad_ctx = grad_ctx.reshape(length, KV_HEADS, group, HEAD_DIM)
    grad_probs = mix("skgh,tkh->kgst", grad_ctx, values_v)
    grad_values = mix("kgst,skgh->tkh", probs, grad_ctx)
    probs_wide = probs.astype(jnp.float32)
    grad_scores = probs_wide * (
        grad_probs - jnp.sum(grad_probs * probs_wide, axis=-1, keepdims=True)
    )
    grad_scores = (grad_scores * HEAD_DIM ** (-0.5)).astype(jnp.bfloat16)
    grad_queries = mix("kgst,tkh->skgh", grad_scores, keys).reshape(length, HEADS, HEAD_DIM)
    grad_keys = mix("kgst,skgh->tkh", grad_scores, grouped)
    grad_joined = jnp.concatenate(
        [
            undo_rope(grad_queries, cosine, sine).reshape(length, inner),
            undo_rope(grad_keys, cosine, sine).reshape(length, kv_width),
            grad_values.reshape(length, kv_width),
        ],
        axis=1,
    ).astype(jnp.bfloat16)
    grad_normed = mix("sj,dj->sd", grad_joined, w_qkv)
    scaled = grad_normed * gain.astype(jnp.float32)
    grad_x = scale_inv * scaled - values * scale_inv**3 * jnp.mean(
        scaled * values, axis=-1, keepdims=True
    )
    grad_x = grad_x + grad_in.astype(jnp.float32)
    return (grad_x.astype(jnp.bfloat16), grad_joined)


def staged(inputs, cotangent, gains, w_qkv, w_out):
    section_count = lax.axis_size("pp")
    section_index = lax.axis_index("pp")
    full_qkv, full_out, full_gain = (
        lax.all_gather(w_qkv[0], "fsdp", axis=0, tiled=True),
        lax.all_gather(w_out[0], "fsdp", axis=0, tiled=True),
        lax.all_gather(gains[0], "fsdp", axis=0, tiled=True),
    )
    micro_count, length, width = inputs.shape
    joined_width = full_qkv.shape[1]
    inner = full_out.shape[1]
    tick_count = micro_count + section_count - 1
    last_section = section_count - 1
    cosine, sine = rope_tables(length)

    def forward_tick(carry, tick):
        received, saved_in, outputs = carry
        slot = tick - section_index
        valid = jnp.logical_and(slot >= 0, slot < micro_count)
        slot_index = jnp.clip(slot, 0, micro_count - 1)
        first_in = lax.dynamic_index_in_dim(inputs, slot_index, 0, keepdims=False)
        layer_in = jnp.where(section_index == 0, first_in, received)

        def forward_run_layer(operands):
            current, kept_in, kept_out = operands
            layer_out = layer_forward(current, full_gain, full_qkv, full_out, cosine, sine)[0]
            kept_in = lax.dynamic_update_index_in_dim(kept_in, current, slot_index, 0)
            kept_out = lax.dynamic_update_index_in_dim(kept_out, layer_out, slot_index, 0)
            return (layer_out, kept_in, kept_out)

        def forward_skip_layer(operands):
            current, kept_in, kept_out = operands
            return (jnp.zeros_like(current), kept_in, kept_out)

        layer_out, saved_in, outputs = lax.cond(
            valid, forward_run_layer, forward_skip_layer, (layer_in, saved_in, outputs)
        )
        received = shifted(layer_out, "pp", 1)
        return ((received, saved_in, outputs), None)

    blank = jnp.zeros((micro_count, length, width), jnp.bfloat16)
    start_carry = (jnp.zeros((length, width), jnp.bfloat16), blank, blank)
    (_, saved_in, outputs), _ = lax.scan(forward_tick, start_carry, jnp.arange(tick_count))
    extra = (
        blank,
        jnp.zeros((micro_count, length, inner), jnp.bfloat16),
        jnp.zeros((micro_count, length, joined_width), jnp.bfloat16),
        blank,
    )

    def backward_tick(carry, tick):
        received, kept = carry
        slot = tick - (last_section - section_index)
        valid = jnp.logical_and(slot >= 0, slot < micro_count)
        slot_index = jnp.clip(slot, 0, micro_count - 1)
        last_in = lax.dynamic_index_in_dim(cotangent, slot_index, 0, keepdims=False)
        grad_in = jnp.where(section_index == last_section, last_in, received)

        def backward_run_layer(operands):
            current, store = operands
            layer_in = lax.dynamic_index_in_dim(saved_in, slot_index, 0, keepdims=False)
            saved = layer_forward(layer_in, full_gain, full_qkv, full_out, cosine, sine)[1]
            grad_x, grad_joined = layer_backward(
                current, saved, full_gain, full_qkv, full_out, cosine, sine
            )
            pieces = (saved[2], saved[7], grad_joined, current)
            store = tuple(
                (
                    lax.dynamic_update_index_in_dim(buffer, piece, slot_index, 0)
                    for buffer, piece in zip(store, pieces)
                )
            )
            return (grad_x, store)

        def backward_skip_layer(operands):
            current, store = operands
            return (jnp.zeros_like(current), store)

        grad_x, kept = lax.cond(valid, backward_run_layer, backward_skip_layer, (grad_in, kept))
        received = shifted(grad_x, "pp", -1)
        return ((received, kept), None)

    (_, extra), _ = lax.scan(
        backward_tick, (jnp.zeros((length, width), jnp.bfloat16), extra), jnp.arange(tick_count)
    )
    normed_all, context_all, joined_all, incoming_all = extra
    summed = lax.psum_scatter(
        jnp.concatenate(
            [
                mix("msd,msj->dj", normed_all, joined_all),
                mix("msd,msc->dc", incoming_all, context_all),
            ],
            axis=1,
        ).astype(jnp.bfloat16),
        "fsdp",
        scatter_dimension=0,
        tiled=True,
    ).astype(jnp.float32)
    grad_qkv = summed[:, :joined_width]
    grad_out = summed[:, joined_width:]
    grad_gain = jnp.sum(grad_qkv * w_qkv[0].astype(jnp.float32), axis=1) / gains[0].astype(
        jnp.float32
    )
    return (outputs[None], grad_qkv[None], grad_out[None], grad_gain[None])


def place(count):
    me = lax.axis_index("fsdp")
    return (count // 4, me // 4, (me // 2) % 2, me % 2)


def at(outer, side, core):
    return (outer * 2 + side) * 2 + core


def remote(source, target, send_sem, recv_sem, device):
    return pltpu.make_async_remote_copy(
        src_ref=source,
        dst_ref=target,
        send_sem=send_sem,
        recv_sem=recv_sem,
        device_id={"fsdp": device},
        device_id_type=MESH,
    )


def greet(outers, outer, side, core):
    barrier = pltpu.get_barrier_semaphore()
    peers = [at((outer + step) % outers, side, core) for step in range(1, outers)]
    peers += [at(outer, 1 - side, core), at(outer, side, 1 - core)]
    for peer in peers:
        pl.semaphore_signal(barrier, inc=1, device_id={"fsdp": peer}, device_id_type=MESH)
    pl.semaphore_wait(barrier, len(peers))


def gather_kernel(
    count, qkv, out, gain, full_qkv, full_out, full_gain, own, z_out, z_in, x_out, x_in, c_out, c_in
):
    outers, outer, side, core = place(count)
    greet(outers, outer, side, core)
    parts = [(gain, full_gain, 0, gain.shape[0])]
    for source, target in ((qkv, full_qkv), (out, full_out)):
        half = source.shape[0] // 2
        parts += [(source, target, 0, half), (source, target, half, half)]
    beside, partner = at(outer, 1 - side, core), at(outer, side, 1 - core)

    def rows(part, owner):
        source, target, start, size = part
        first = pl.multiple_of(owner * source.shape[0] + start, 16)
        return target.at[pl.ds(first, size)]

    started, local = [], []

    def send(source, target, send_sem, recv_sem, device):
        copy = remote(source, target, send_sem, recv_sem, device)
        copy.start()
        started.append(copy)

    for j, part in enumerate(parts):
        source, target, start, size = part
        block, spot = source.at[pl.ds(start, size)], rows(part, at(outer, side, core))
        for step in range(1, outers):
            peer = at((outer + step) % outers, side, core)
            send(block, spot, z_out.at[step, j], z_in.at[step, j], peer)
        send(block, spot, x_out.at[0, j], x_in.at[0, j], beside)
        send(block, spot, c_out.at[0, 0, j], c_in.at[0, 0, j], partner)
        copy = pltpu.make_async_copy(block, spot, own.at[j])
        copy.start()
        local.append(copy)
    for j, part in enumerate(parts):
        for step in range(1, outers):
            spot = rows(part, at((outer + outers - step) % outers, side, core))
            remote(spot, spot, z_out.at[step, j], z_in.at[step, j], beside).wait_recv()
            send(spot, spot, x_out.at[step, j], x_in.at[step, j], beside)
            send(spot, spot, c_out.at[0, step, j], c_in.at[0, step, j], partner)
        for step in range(outers):
            spot = rows(part, at((outer + outers - step) % outers, 1 - side, core))
            remote(spot, spot, x_out.at[step, j], x_in.at[step, j], beside).wait_recv()
            send(spot, spot, c_out.at[1, step, j], c_in.at[1, step, j], partner)
    for j, part in enumerate(parts):
        for over in range(2):
            for step in range(outers):
                origin = at(
                    (outer + outers - step) % outers, 1 - side if over else side, 1 - core
                )
                spot = rows(part, origin)
                remote(
                    spot, spot, c_out.at[over, step, j], c_in.at[over, step, j], partner
                ).wait_recv()
    for copy in started:
        copy.wait_send()
    for copy in local:
        copy.wait()


def gather(qkv, out, gain):
    count = lax.axis_size("fsdp")
    outers = count // 4
    gain = jnp.broadcast_to(gain[None], (16, gain.shape[0]))
    sems = [(outers, 5), (outers, 5), (outers, 5), (outers, 5), (2, outers, 5), (2, outers, 5)]
    full_qkv, full_out, full_gain = pl.pallas_call(
        functools.partial(gather_kernel, count),
        out_shape=[
            jax.ShapeDtypeStruct((count * block.shape[0], block.shape[1]), block.dtype)
            for block in (qkv, out, gain)
        ],
        in_specs=[pl.BlockSpec(memory_space=pl.ANY)] * 3,
        out_specs=[pl.BlockSpec(memory_space=pl.ANY)] * 3,
        scratch_shapes=[pltpu.SemaphoreType.DMA((5,))]
        + [pltpu.SemaphoreType.DMA(shape) for shape in sems],
        compiler_params=pltpu.CompilerParams(collective_id=0, has_side_effects=True),
    )(qkv, out, gain)
    return (full_qkv, full_out, full_gain.reshape(count, 16, -1)[:, 0].reshape(-1))


def reduce_kernel(
    count, normed, joined, incoming, context, sum_qkv, sum_out,
    c_buf, own, c_got, x_buf, x_got, z_buf, z_got, c_out, c_in, x_out, x_in, z_out, z_in,
):
    outers, outer, side, core = place(count)
    depth, width = sum_qkv.shape
    beside, partner = at(outer, 1 - side, core), at(outer, side, 1 - core)
    greet(outers, outer, side, core)

    def term(index, target):
        columns = pl.ds(pl.multiple_of(index * depth, depth), depth)
        form = (((0,), (0,)), ((), ()))
        target[:, :width] = lax.dot_general(
            normed[:, columns], joined[...], form, preferred_element_type=jnp.float32
        ).astype(jnp.bfloat16)
        target[:, width:] = lax.dot_general(
            incoming[:, columns], context[...], form, preferred_element_type=jnp.float32
        ).astype(jnp.bfloat16)

    def to_core(k):
        return remote(c_buf.at[k], c_got.at[k], c_out.at[k], c_in.at[k], partner)

    def to_side(k):
        return remote(x_buf.at[k], x_got.at[k], x_out.at[k], x_in.at[k], beside)

    def to_outer(k):
        peer = at((outer + k + 1) % outers, side, core)
        return remote(z_buf.at[k], z_got.at[k], z_out.at[k], z_in.at[k], peer)

    def wide(ref):
        return ref[...].astype(jnp.float32)

    def combine(k):
        to_core(k).wait_recv()
        both = (wide(own.at[k]) + wide(c_got.at[k])).astype(jnp.bfloat16)

        @pl.when(k < outers)
        def _():
            x_buf[k % outers] = both
            to_side(k % outers).start()

        @pl.when(k >= outers)
        def _():
            own[k] = both

    def one(k, carry):
        where = (outer + k + 1) % outers
        over = k // outers
        there = over * side + (1 - over) * (1 - side)
        term(at(where, there, 1 - core), c_buf.at[k])
        to_core(k).start()
        term(at(where, there, core), own.at[k])

        @pl.when(k > 0)
        def _():
            combine(k - 1)

        return carry

    lax.fori_loop(0, 2 * outers, one, 0)
    combine(2 * outers - 1)

    def two(k, carry):
        to_side(k).wait_recv()
        z_buf[k] = (wide(own.at[outers + k]) + wide(x_got.at[k])).astype(jnp.bfloat16)
        to_outer(k).start()
        return carry

    lax.fori_loop(0, outers - 1, two, 0)
    last = outers - 1
    to_side(last).wait_recv()
    total = wide(own.at[outers + last]) + wide(x_got.at[last])
    for k in range(last):
        to_outer(k).wait_recv()
        total += wide(z_got.at[k])
    sum_qkv[...] = total[:, :width]
    sum_out[...] = total[:, width:]

    for k in range(2 * outers):
        to_core(k).wait_send()
    for k in range(outers):
        to_side(k).wait_send()
    for k in range(last):
        to_outer(k).wait_send()


def reduce_terms(normed, joined, incoming, context):
    count = lax.axis_size("fsdp")
    outers = count // 4
    tokens, width = normed.shape
    depth = width // count
    columns = joined.shape[1] + context.shape[1]

    def slots(number):
        return pltpu.VMEM((number, depth, columns), jnp.bfloat16)

    numbers = (2 * outers, 2 * outers, 2 * outers, outers, outers, outers - 1, outers - 1)
    sems = (2 * outers, 2 * outers, outers, outers, outers - 1, outers - 1)
    return pl.pallas_call(
        functools.partial(reduce_kernel, count),
        out_shape=[
            jax.ShapeDtypeStruct((depth, piece.shape[1]), jnp.float32) for piece in (joined, context)
        ],
        in_specs=[pl.BlockSpec(memory_space=pltpu.VMEM)] * 4,
        out_specs=[pl.BlockSpec(memory_space=pltpu.VMEM)] * 2,
        scratch_shapes=[slots(number) for number in numbers]
        + [pltpu.SemaphoreType.DMA((number,)) for number in sems],
        compiler_params=pltpu.CompilerParams(
            collective_id=1, has_side_effects=True, vmem_limit_bytes=48 * 1024 * 1024
        ),
    )(normed, joined, incoming, context)


NT = (((1,), (1,)), ((), ()))
TN = (((0,), (0,)), ((), ()))


def dot(left, right, form=(((1,), (0,)), ((), ()))):
    return lax.dot_general(left, right, form, preferred_element_type=jnp.float32)


def turned(values, signed):
    lane = lax.broadcasted_iota(jnp.int32, values.shape, 1) % HEAD_DIM
    ahead = pltpu.roll(values, 2 * HEAD_DIM - HEAD_DIM // 2, 1)
    behind = pltpu.roll(values, HEAD_DIM // 2, 1)
    return jnp.where(lane < HEAD_DIM // 2, ahead, behind) * signed


def heads(ref, group, kv):
    first = kv * group
    return jnp.concatenate(
        [ref[:, h * HEAD_DIM : (h + 1) * HEAD_DIM] for h in range(first, first + group)], axis=0
    )


def norm_scale(values):
    return lax.rsqrt(jnp.mean(values * values, axis=1, keepdims=True) + 1e-05)


def forward_kernel(x, gain, w_qkv, w_out, cosine, signed, out, normed, qkv, probs, context, joined):
    length = x.shape[0]
    group, inner, kv_width = HEADS // KV_HEADS, HEADS * HEAD_DIM, KV_HEADS * HEAD_DIM
    values = x[...].astype(jnp.float32)
    normed[...] = (values * norm_scale(values) * gain[...]).astype(jnp.bfloat16)
    joined[...] = dot(normed[...], w_qkv[...])
    pair = 2 * HEAD_DIM
    for first in range(0, inner + kv_width, pair):
        block = joined[:, first : first + pair]
        qkv[:, first : first + pair] = (
            block * cosine[...] + turned(block, signed[...])
        ).astype(jnp.bfloat16)
    qkv[:, inner + kv_width :] = joined[:, inner + kv_width :].astype(jnp.bfloat16)
    shape = (group * length, length)
    row = lax.broadcasted_iota(jnp.int32, shape, 0) % length
    causal = row >= lax.broadcasted_iota(jnp.int32, shape, 1)
    for kv in range(KV_HEADS):
        start = inner + kv * HEAD_DIM
        key = qkv[:, start : start + HEAD_DIM]
        value = qkv[:, start + kv_width : start + kv_width + HEAD_DIM]
        scores = dot(heads(qkv, group, kv), key, NT) * HEAD_DIM ** (-0.5)
        weights = jnp.where(causal, jnp.exp(scores), 0.0)
        rounded = (weights * (1.0 / jnp.sum(weights, axis=1, keepdims=True))).astype(jnp.bfloat16)
        probs[kv] = rounded
        mixed = dot(rounded, value).astype(jnp.bfloat16)
        for h in range(group):
            first = (kv * group + h) * HEAD_DIM
            context[:, first : first + HEAD_DIM] = mixed[h * length : (h + 1) * length]
    out[...] = (x[...].astype(jnp.float32) + dot(context[...], w_out[...], NT)).astype(jnp.bfloat16)


def backward_kernel(
    grad_in, x, gain, w_qkv, w_out, cosine, signed, qkv, probs, grad_x, grad_joined, wide, grad_ctx
):
    length = x.shape[0]
    group, inner, kv_width = HEADS // KV_HEADS, HEADS * HEAD_DIM, KV_HEADS * HEAD_DIM
    grad_ctx[...] = dot(grad_in[...], w_out[...]).astype(jnp.bfloat16)
    for kv in range(KV_HEADS):
        start = inner + kv * HEAD_DIM
        key = qkv[:, start : start + HEAD_DIM]
        value = qkv[:, start + kv_width : start + kv_width + HEAD_DIM]
        from_ctx = heads(grad_ctx, group, kv)
        kept = probs[kv].astype(jnp.float32)
        grad_probs = dot(from_ctx, value, NT)
        wide[:, start + kv_width : start + kv_width + HEAD_DIM] = dot(probs[kv], from_ctx, TN)
        centred = grad_probs - jnp.sum(grad_probs * kept, axis=1, keepdims=True)
        grad_scores = (kept * centred * HEAD_DIM ** (-0.5)).astype(jnp.bfloat16)
        grad_query = dot(grad_scores, key)
        for h in range(group):
            first = (kv * group + h) * HEAD_DIM
            wide[:, first : first + HEAD_DIM] = grad_query[h * length : (h + 1) * length]
        wide[:, start : start + HEAD_DIM] = dot(grad_scores, heads(qkv, group, kv), TN)
    pair = 2 * HEAD_DIM
    for first in range(0, inner + kv_width, pair):
        block = wide[:, first : first + pair]
        grad_joined[:, first : first + pair] = (
            block * cosine[...] - turned(block, signed[...])
        ).astype(jnp.bfloat16)
    grad_joined[:, inner + kv_width :] = wide[:, inner + kv_width :].astype(jnp.bfloat16)
    values = x[...].astype(jnp.float32)
    scale_inv = norm_scale(values)
    scaled = dot(grad_joined[...], w_qkv[...], NT) * gain[...]
    centre = scale_inv**3 * jnp.mean(scaled * values, axis=1, keepdims=True)
    total = scale_inv * scaled - values * centre + grad_in[...].astype(jnp.float32)
    grad_x[...] = total.astype(jnp.bfloat16)


def local_call(kernel, flops, results, scratch, operands):
    moved = sum(array.size * array.dtype.itemsize for array in operands)
    return pl.pallas_call(
        kernel,
        out_shape=[jax.ShapeDtypeStruct(shape, jnp.bfloat16) for shape in results],
        in_specs=[pl.BlockSpec(memory_space=pltpu.VMEM)] * len(operands),
        out_specs=[pl.BlockSpec(memory_space=pltpu.VMEM)] * len(results),
        scratch_shapes=scratch,
        cost_estimate=pl.CostEstimate(flops=flops, bytes_accessed=moved, transcendentals=0),
        compiler_params=pltpu.CompilerParams(vmem_limit_bytes=40 * 1024 * 1024),
    )(*operands)


def run_forward(x, weights):
    length, width = x.shape
    columns, inner = weights[1].shape[1], weights[2].shape[1]
    probs = (KV_HEADS, HEADS // KV_HEADS * length, length)
    results = [(length, width), (length, width), (length, columns), probs, (length, inner)]
    scratch = [pltpu.VMEM((length, columns), jnp.float32)]
    flops = 2 * length * width * (columns + inner)
    out, normed, qkv, probs, context = local_call(
        forward_kernel, flops, results, scratch, (x, *weights)
    )
    return (out, x, normed, qkv, probs, context)


def run_backward(grad_in, x, qkv, probs, weights):
    length, width = x.shape
    columns, inner = weights[1].shape[1], weights[2].shape[1]
    scratch = [pltpu.VMEM((length, columns), jnp.float32), pltpu.VMEM((length, inner), jnp.bfloat16)]
    flops = 2 * length * width * (columns + inner)
    results = [(length, width), (length, columns)]
    return local_call(
        backward_kernel, flops, results, scratch, (grad_in, x, *weights, qkv, probs)
    )


def pick(first, own, other):
    return jax.tree.map(lambda left, right: jnp.where(first, left, right), own, other)


def two_sections(inputs, cotangent, gains, w_qkv, w_out):
    first = lax.axis_index("pp") == 0
    full_qkv, full_out, full_gain = gather(w_qkv[0], w_out[0], gains[0])
    micro_count, length, width = inputs.shape
    cosine, sine = rope_tables(length)
    half = HEAD_DIM // 2
    cosine = jnp.concatenate([cosine, cosine], axis=1)
    signed = jnp.concatenate([-sine[:, :half], sine[:, half:]] * 2, axis=1)
    weights = (full_gain.astype(jnp.float32)[None], full_qkv, full_out, cosine, signed)
    early, sent = [], []
    for micro in range(micro_count):
        early.append(run_forward(inputs[micro], weights))
        sent.append(shifted(early[-1][0], "pp", 1))
    late, back = [], []
    for micro in range(micro_count):
        late.append(run_forward(sent[micro], weights))
        _, x, _, qkv, probs, _ = late[-1]
        grad_x = run_backward(cotangent[micro], x, qkv, probs, weights)[0]
        back.append(shifted(grad_x, "pp", -1))
    kept = []
    for micro in range(micro_count):
        out, x, normed, qkv, probs, context = pick(first, early[micro], late[micro])
        grad_in = jnp.where(first, back[micro], cotangent[micro])
        grad_joined = run_backward(grad_in, x, qkv, probs, weights)[1]
        kept.append((out, normed, grad_joined, grad_in, context))
    outputs, normed, joined, incoming, context = zip(*kept)
    return finish(outputs, normed, joined, incoming, context, gains, w_qkv)


def finish(outputs, normed, joined, incoming, context, gains, w_qkv):
    pieces = (jnp.concatenate(piece, axis=0) for piece in (normed, joined, incoming, context))
    grad_qkv, grad_out = reduce_terms(*pieces)
    grad_gain = jnp.sum(grad_qkv * w_qkv[0].astype(jnp.float32), axis=1) / gains[0].astype(
        jnp.float32
    )
    return (jnp.stack(outputs)[None], grad_qkv[None], grad_out[None], grad_gain[None])


def solution(mesh):
    return jax.shard_map(
        two_sections if mesh.shape["pp"] == 2 else staged,
        mesh=mesh,
        in_specs=(
            P(None, "fsdp", None),
            P(None, "fsdp", None),
            P("pp", "fsdp"),
            P("pp", "fsdp", None),
            P("pp", "fsdp", None),
        ),
        out_specs=(
            P("pp", None, "fsdp", None),
            P("pp", "fsdp", None),
            P("pp", "fsdp", None),
            P("pp", "fsdp"),
        ),
        check_vma=False,
    )
```

```python
import functools

import jax
import jax.numpy as jnp
from jax import lax
from jax.experimental import pallas as pl
from jax.experimental.pallas import tpu as pltpu
from jax.sharding import PartitionSpec as P

HEADS = 16
KV_HEADS = 4
HEAD_DIM = 64
MESH = pl.DeviceIdType.MESH
PIECES = 4


def shifted(value, axis, steps):
    count = lax.axis_size(axis)
    leading, last = (max(0, -steps), min(count, count - steps))
    return lax.ppermute(value, axis, [(source, source + steps) for source in range(leading, last)])


def mix(form, left, right):
    return jnp.einsum(form, left, right, preferred_element_type=jnp.float32)


def rope_tables(length):
    positions = jnp.arange(length, dtype=jnp.float32)
    freqs = 500000.0 ** (-jnp.arange(HEAD_DIM // 2, dtype=jnp.float32) * 2.0 / HEAD_DIM)
    angles = positions[:, None] * freqs[None, :]
    cosine = jnp.concatenate([jnp.cos(angles), jnp.cos(angles)], axis=1)
    sine = jnp.concatenate([jnp.sin(angles), jnp.sin(angles)], axis=1)
    return (cosine, sine)


def rotate_half(values):
    first = values[..., : HEAD_DIM // 2]
    second = values[..., HEAD_DIM // 2 :]
    return jnp.concatenate([-second, first], axis=-1)


def apply_rope(values, cosine, sine):
    return values * cosine[:, None, :] + rotate_half(values) * sine[:, None, :]


def undo_rope(grads, cosine, sine):
    return grads * cosine[:, None, :] - rotate_half(grads * sine[:, None, :])


def layer_forward(layer_in, gain, w_qkv, w_out, cosine, sine):
    length = layer_in.shape[0]
    group = HEADS // KV_HEADS
    inner = HEADS * HEAD_DIM
    kv_width = KV_HEADS * HEAD_DIM
    values = layer_in.astype(jnp.float32)
    scale_inv = lax.rsqrt(jnp.mean(values * values, axis=-1, keepdims=True) + 1e-05)
    normed = (values * scale_inv * gain.astype(jnp.float32)).astype(jnp.bfloat16)
    joined = jnp.dot(normed, w_qkv, preferred_element_type=jnp.float32)
    queries = apply_rope(joined[:, :inner].reshape(length, HEADS, HEAD_DIM), cosine, sine).astype(
        jnp.bfloat16
    )
    keys = apply_rope(
        joined[:, inner : inner + kv_width].reshape(length, KV_HEADS, HEAD_DIM), cosine, sine
    ).astype(jnp.bfloat16)
    values_v = (
        joined[:, inner + kv_width :].reshape(length, KV_HEADS, HEAD_DIM).astype(jnp.bfloat16)
    )
    grouped = queries.reshape(length, KV_HEADS, group, HEAD_DIM)
    scores = mix("skgh,tkh->kgst", grouped, keys) * HEAD_DIM ** (-0.5)
    causal = jnp.arange(length)[:, None] >= jnp.arange(length)[None, :]
    weights = jnp.where(causal, jnp.exp(scores), 0.0)
    probs = (weights / jnp.sum(weights, axis=-1, keepdims=True)).astype(jnp.bfloat16)
    context = mix("kgst,tkh->skgh", probs, values_v).reshape(length, inner).astype(jnp.bfloat16)
    mixed = values + mix("sc,dc->sd", context, w_out)
    saved = (values, scale_inv, normed, grouped, keys, values_v, probs, context)
    return (mixed.astype(jnp.bfloat16), saved)


def layer_backward(grad_in, saved, gain, w_qkv, w_out, cosine, sine):
    values, scale_inv, normed, grouped, keys, values_v, probs, context = saved
    length = grad_in.shape[0]
    group = HEADS // KV_HEADS
    inner = HEADS * HEAD_DIM
    kv_width = KV_HEADS * HEAD_DIM
    grad_ctx = jnp.dot(grad_in, w_out, preferred_element_type=jnp.float32).astype(jnp.bfloat16)
    grad_ctx = grad_ctx.reshape(length, KV_HEADS, group, HEAD_DIM)
    grad_probs = mix("skgh,tkh->kgst", grad_ctx, values_v)
    grad_values = mix("kgst,skgh->tkh", probs, grad_ctx)
    probs_wide = probs.astype(jnp.float32)
    grad_scores = probs_wide * (
        grad_probs - jnp.sum(grad_probs * probs_wide, axis=-1, keepdims=True)
    )
    grad_scores = (grad_scores * HEAD_DIM ** (-0.5)).astype(jnp.bfloat16)
    grad_queries = mix("kgst,tkh->skgh", grad_scores, keys).reshape(length, HEADS, HEAD_DIM)
    grad_keys = mix("kgst,skgh->tkh", grad_scores, grouped)
    grad_joined = jnp.concatenate(
        [
            undo_rope(grad_queries, cosine, sine).reshape(length, inner),
            undo_rope(grad_keys, cosine, sine).reshape(length, kv_width),
            grad_values.reshape(length, kv_width),
        ],
        axis=1,
    ).astype(jnp.bfloat16)
    grad_normed = mix("sj,dj->sd", grad_joined, w_qkv)
    scaled = grad_normed * gain.astype(jnp.float32)
    grad_x = scale_inv * scaled - values * scale_inv**3 * jnp.mean(
        scaled * values, axis=-1, keepdims=True
    )
    grad_x = grad_x + grad_in.astype(jnp.float32)
    return (grad_x.astype(jnp.bfloat16), grad_joined)


def staged(inputs, cotangent, gains, w_qkv, w_out):
    section_count = lax.axis_size("pp")
    section_index = lax.axis_index("pp")
    full_qkv, full_out, full_gain = (
        lax.all_gather(w_qkv[0], "fsdp", axis=0, tiled=True),
        lax.all_gather(w_out[0], "fsdp", axis=0, tiled=True),
        lax.all_gather(gains[0], "fsdp", axis=0, tiled=True),
    )
    micro_count, length, width = inputs.shape
    joined_width = full_qkv.shape[1]
    inner = full_out.shape[1]
    tick_count = micro_count + section_count - 1
    last_section = section_count - 1
    cosine, sine = rope_tables(length)

    def forward_tick(carry, tick):
        received, saved_in, outputs = carry
        slot = tick - section_index
        valid = jnp.logical_and(slot >= 0, slot < micro_count)
        slot_index = jnp.clip(slot, 0, micro_count - 1)
        first_in = lax.dynamic_index_in_dim(inputs, slot_index, 0, keepdims=False)
        layer_in = jnp.where(section_index == 0, first_in, received)

        def forward_run_layer(operands):
            current, kept_in, kept_out = operands
            layer_out = layer_forward(current, full_gain, full_qkv, full_out, cosine, sine)[0]
            kept_in = lax.dynamic_update_index_in_dim(kept_in, current, slot_index, 0)
            kept_out = lax.dynamic_update_index_in_dim(kept_out, layer_out, slot_index, 0)
            return (layer_out, kept_in, kept_out)

        def forward_skip_layer(operands):
            current, kept_in, kept_out = operands
            return (jnp.zeros_like(current), kept_in, kept_out)

        layer_out, saved_in, outputs = lax.cond(
            valid, forward_run_layer, forward_skip_layer, (layer_in, saved_in, outputs)
        )
        received = shifted(layer_out, "pp", 1)
        return ((received, saved_in, outputs), None)

    blank = jnp.zeros((micro_count, length, width), jnp.bfloat16)
    start_carry = (jnp.zeros((length, width), jnp.bfloat16), blank, blank)
    (_, saved_in, outputs), _ = lax.scan(forward_tick, start_carry, jnp.arange(tick_count))
    extra = (
        blank,
        jnp.zeros((micro_count, length, inner), jnp.bfloat16),
        jnp.zeros((micro_count, length, joined_width), jnp.bfloat16),
        blank,
    )

    def backward_tick(carry, tick):
        received, kept = carry
        slot = tick - (last_section - section_index)
        valid = jnp.logical_and(slot >= 0, slot < micro_count)
        slot_index = jnp.clip(slot, 0, micro_count - 1)
        last_in = lax.dynamic_index_in_dim(cotangent, slot_index, 0, keepdims=False)
        grad_in = jnp.where(section_index == last_section, last_in, received)

        def backward_run_layer(operands):
            current, store = operands
            layer_in = lax.dynamic_index_in_dim(saved_in, slot_index, 0, keepdims=False)
            saved = layer_forward(layer_in, full_gain, full_qkv, full_out, cosine, sine)[1]
            grad_x, grad_joined = layer_backward(
                current, saved, full_gain, full_qkv, full_out, cosine, sine
            )
            pieces = (saved[2], saved[7], grad_joined, current)
            store = tuple(
                (
                    lax.dynamic_update_index_in_dim(buffer, piece, slot_index, 0)
                    for buffer, piece in zip(store, pieces)
                )
            )
            return (grad_x, store)

        def backward_skip_layer(operands):
            current, store = operands
            return (jnp.zeros_like(current), store)

        grad_x, kept = lax.cond(valid, backward_run_layer, backward_skip_layer, (grad_in, kept))
        received = shifted(grad_x, "pp", -1)
        return ((received, kept), None)

    (_, extra), _ = lax.scan(
        backward_tick, (jnp.zeros((length, width), jnp.bfloat16), extra), jnp.arange(tick_count)
    )
    normed_all, context_all, joined_all, incoming_all = extra
    summed = lax.psum_scatter(
        jnp.concatenate(
            [
                mix("msd,msj->dj", normed_all, joined_all),
                mix("msd,msc->dc", incoming_all, context_all),
            ],
            axis=1,
        ).astype(jnp.bfloat16),
        "fsdp",
        scatter_dimension=0,
        tiled=True,
    ).astype(jnp.float32)
    grad_qkv = summed[:, :joined_width]
    grad_out = summed[:, joined_width:]
    grad_gain = jnp.sum(grad_qkv * w_qkv[0].astype(jnp.float32), axis=1) / gains[0].astype(
        jnp.float32
    )
    return (outputs[None], grad_qkv[None], grad_out[None], grad_gain[None])


def place(count):
    me = lax.axis_index("fsdp")
    return (count // 4, me // 4, (me // 2) % 2, me % 2)


def at(outer, side, core):
    return (outer * 2 + side) * 2 + core


def remote(source, target, send_sem, recv_sem, device):
    return pltpu.make_async_remote_copy(
        src_ref=source,
        dst_ref=target,
        send_sem=send_sem,
        recv_sem=recv_sem,
        device_id={"fsdp": device},
        device_id_type=MESH,
    )


def greet(outers, outer, side, core):
    barrier = pltpu.get_barrier_semaphore()
    peers = [at((outer + step) % outers, side, core) for step in range(1, outers)]
    peers += [at(outer, 1 - side, core), at(outer, side, 1 - core)]
    for peer in peers:
        pl.semaphore_signal(barrier, inc=1, device_id={"fsdp": peer}, device_id_type=MESH)
    pl.semaphore_wait(barrier, len(peers))


def gather_kernel(
    count, qkv, out, gain, full_qkv, full_out, full_gain, own, z_out, z_in, x_out, x_in, c_out, c_in
):
    outers, outer, side, core = place(count)
    greet(outers, outer, side, core)
    parts = [(gain, full_gain, 0, gain.shape[0])]
    for source, target in ((qkv, full_qkv), (out, full_out)):
        size = source.shape[0] // 4
        parts += [(source, target, k * size, size) for k in range(4)]
    beside, partner = at(outer, 1 - side, core), at(outer, side, 1 - core)

    def rows(part, owner):
        source, target, start, size = part
        first = pl.multiple_of(owner * source.shape[0] + start, 16)
        return target.at[pl.ds(first, size)]

    def origin(way, step):
        return outer + step if way else outer - step

    def known(way, step):
        return outer + step < outers if way else outer >= step

    def onward(way, step, j, source, target):
        ahead = outer - 1 if way else outer + 1
        device = at((ahead + outers) % outers, side, core)
        sent, got = z_out.at[way, step, j], z_in.at[way, step + 1, j]
        return remote(source, target, sent, got, device)

    def across(way, step, j, source, target):
        return remote(source, target, x_out.at[way, step, j], x_in.at[way, step, j], beside)

    def paired(over, way, step, j, source, target):
        sent, got = c_out.at[over, way, step, j], c_in.at[over, way, step, j]
        return remote(source, target, sent, got, partner)

    def can_pass(way):
        return outer >= 1 if way else outer + 1 < outers

    hops = [(way, step) for step in range(1, outers) for way in range(2)]
    for j, part in enumerate(parts):
        source, target, start, size = part
        block, spot = source.at[pl.ds(start, size)], rows(part, at(outer, side, core))
        for way in range(2):
            pl.when(can_pass(way))(onward(way, 0, j, block, spot).start)
        across(0, 0, j, block, spot).start()
        paired(0, 0, 0, j, block, spot).start()
        pltpu.make_async_copy(block, spot, own.at[j]).start()
    for j, part in enumerate(parts):
        for way, step in hops:

            @pl.when(known(way, step))
            def _(way=way, step=step, j=j, part=part):
                spot = rows(part, at(origin(way, step), side, core))
                onward(way, step - 1, j, spot, spot).wait_recv()
                if step < outers - 1:
                    pl.when(can_pass(way))(onward(way, step, j, spot, spot).start)
                across(way, step, j, spot, spot).start()
                paired(0, way, step, j, spot, spot).start()

        for way, step in [(0, 0)] + hops:

            @pl.when(known(way, step))
            def _(way=way, step=step, j=j, part=part):
                spot = rows(part, at(origin(way, step), 1 - side, core))
                across(way, step, j, spot, spot).wait_recv()
                paired(1, way, step, j, spot, spot).start()

    for j, part in enumerate(parts):
        for way, step in [(0, 0), (1, 0)] + hops:

            @pl.when(known(way, step))
            def _(way=way, step=step, j=j, part=part):
                spot = rows(part, at(origin(way, step), side, core))
                if step < outers - 1:
                    pl.when(can_pass(way))(onward(way, step, j, spot, spot).wait_send)
                if (way, step) == (1, 0):
                    return
                across(way, step, j, spot, spot).wait_send()
                for over in range(2):
                    there = 1 - side if over else side
                    landed = rows(part, at(origin(way, step), there, 1 - core))
                    copy = paired(over, way, step, j, landed, landed)
                    copy.wait_recv()
                    copy.wait_send()

        source, target, start, size = part
        block, spot = source.at[pl.ds(start, size)], rows(part, at(outer, side, core))
        pltpu.make_async_copy(block, spot, own.at[j]).wait()


def gather(qkv, out, gain):
    count = lax.axis_size("fsdp")
    outers = count // 4
    gain = jnp.broadcast_to(gain[None], (16, gain.shape[0]))
    sems = [(2, outers, 9)] * 4 + [(2, 2, outers, 9)] * 2
    full_qkv, full_out, full_gain = pl.pallas_call(
        functools.partial(gather_kernel, count),
        out_shape=[
            jax.ShapeDtypeStruct((count * block.shape[0], block.shape[1]), block.dtype)
            for block in (qkv, out, gain)
        ],
        in_specs=[pl.BlockSpec(memory_space=pl.ANY)] * 3,
        out_specs=[pl.BlockSpec(memory_space=pl.ANY)] * 3,
        scratch_shapes=[pltpu.SemaphoreType.DMA((9,))]
        + [pltpu.SemaphoreType.DMA(shape) for shape in sems],
        compiler_params=pltpu.CompilerParams(collective_id=0, has_side_effects=True),
    )(qkv, out, gain)
    return (full_qkv, full_out, full_gain.reshape(count, 16, -1)[:, 0].reshape(-1))


def reduce_kernel(
    count, normed, joined, incoming, context, sum_qkv, sum_out,
    c_buf, own, c_got, x_buf, x_got, z_buf, z_got, c_out, c_in, x_out, x_in, z_out, z_in,
):
    outers, outer, side, core = place(count)
    depth, width = sum_qkv.shape
    beside, partner = at(outer, 1 - side, core), at(outer, side, 1 - core)
    greet(outers, outer, side, core)

    def term(index, target):
        columns = pl.ds(pl.multiple_of(index * depth, depth), depth)
        form = (((0,), (0,)), ((), ()))
        target[:, :width] = lax.dot_general(
            normed[:, columns], joined[...], form, preferred_element_type=jnp.float32
        ).astype(jnp.bfloat16)
        target[:, width:] = lax.dot_general(
            incoming[:, columns], context[...], form, preferred_element_type=jnp.float32
        ).astype(jnp.bfloat16)

    def to_core(k):
        return remote(c_buf.at[k], c_got.at[k], c_out.at[k], c_in.at[k], partner)

    part = (width + context.shape[1]) // PIECES

    def cut(p):
        return slice(p * part, (p + 1) * part)

    def to_side(k, p):
        source, target = x_buf.at[k, :, cut(p)], x_got.at[k, :, cut(p)]
        return remote(source, target, x_out.at[k, p], x_in.at[k, p], beside)

    def to_outer(k, p):
        peer = at((outer + k + 1) % outers, side, core)
        source, target = z_buf.at[k, :, cut(p)], z_got.at[k, :, cut(p)]
        return remote(source, target, z_out.at[k, p], z_in.at[k, p], peer)

    def wide(ref):
        return ref[...].astype(jnp.float32)

    def combine(k):
        to_core(k).wait_recv()
        both = (wide(own.at[k]) + wide(c_got.at[k])).astype(jnp.bfloat16)

        @pl.when(k < outers)
        def _():
            x_buf[k % outers] = both
            for p in range(PIECES):
                to_side(k % outers, p).start()

        @pl.when(k >= outers)
        def _():
            own[k] = both

    def one(k, carry):
        where = (outer + k + 1) % outers
        over = k // outers
        there = over * side + (1 - over) * (1 - side)
        term(at(where, there, 1 - core), c_buf.at[k])
        to_core(k).start()
        term(at(where, there, core), own.at[k])

        @pl.when(k > 0)
        def _():
            combine(k - 1)

        return carry

    lax.fori_loop(0, 2 * outers, one, 0)
    combine(2 * outers - 1)

    def two(k, carry):
        for p in range(PIECES):
            to_side(k, p).wait_recv()
            z_buf[k, :, cut(p)] = (
                own[outers + k, :, cut(p)].astype(jnp.float32)
                + x_got[k, :, cut(p)].astype(jnp.float32)
            ).astype(jnp.bfloat16)
            to_outer(k, p).start()
        return carry

    lax.fori_loop(0, outers - 1, two, 0)
    last = outers - 1
    for p in range(PIECES):
        to_side(last, p).wait_recv()
        for k in range(last):
            to_outer(k, p).wait_recv()
    total = wide(own.at[outers + last]) + wide(x_got.at[last])
    for k in range(last):
        total += wide(z_got.at[k])
    sum_qkv[...] = total[:, :width]
    sum_out[...] = total[:, width:]

    for k in range(2 * outers):
        to_core(k).wait_send()
    for p in range(PIECES):
        for k in range(outers):
            to_side(k, p).wait_send()
        for k in range(last):
            to_outer(k, p).wait_send()


def reduce_terms(normed, joined, incoming, context):
    count = lax.axis_size("fsdp")
    outers = count // 4
    tokens, width = normed.shape
    depth = width // count
    columns = joined.shape[1] + context.shape[1]

    def slots(number):
        return pltpu.VMEM((number, depth, columns), jnp.bfloat16)

    numbers = (2 * outers, 2 * outers, 2 * outers, outers, outers, outers - 1, outers - 1)
    sems = [(2 * outers,)] * 2 + [(outers, PIECES)] * 2 + [(outers - 1, PIECES)] * 2
    return pl.pallas_call(
        functools.partial(reduce_kernel, count),
        out_shape=[
            jax.ShapeDtypeStruct((depth, piece.shape[1]), jnp.float32) for piece in (joined, context)
        ],
        in_specs=[pl.BlockSpec(memory_space=pltpu.VMEM)] * 4,
        out_specs=[pl.BlockSpec(memory_space=pltpu.VMEM)] * 2,
        scratch_shapes=[slots(number) for number in numbers]
        + [pltpu.SemaphoreType.DMA(shape) for shape in sems],
        compiler_params=pltpu.CompilerParams(
            collective_id=1, has_side_effects=True, vmem_limit_bytes=48 * 1024 * 1024
        ),
    )(normed, joined, incoming, context)


NT = (((1,), (1,)), ((), ()))
TN = (((0,), (0,)), ((), ()))


def dot(left, right, form=(((1,), (0,)), ((), ()))):
    return lax.dot_general(left, right, form, preferred_element_type=jnp.float32)


def turned(values, signed):
    lane = lax.broadcasted_iota(jnp.int32, values.shape, 1) % HEAD_DIM
    ahead = pltpu.roll(values, 2 * HEAD_DIM - HEAD_DIM // 2, 1)
    behind = pltpu.roll(values, HEAD_DIM // 2, 1)
    return jnp.where(lane < HEAD_DIM // 2, ahead, behind) * signed


def heads(ref, group, kv):
    first = kv * group
    return jnp.concatenate(
        [ref[:, h * HEAD_DIM : (h + 1) * HEAD_DIM] for h in range(first, first + group)], axis=0
    )


def norm_scale(values):
    return lax.rsqrt(jnp.mean(values * values, axis=1, keepdims=True) + 1e-05)


def forward_kernel(x, gain, w_qkv, w_out, cosine, signed, out, normed, qkv, probs, context, joined):
    length = x.shape[0]
    group, inner, kv_width = HEADS // KV_HEADS, HEADS * HEAD_DIM, KV_HEADS * HEAD_DIM
    values = x[...].astype(jnp.float32)
    normed[...] = (values * norm_scale(values) * gain[...]).astype(jnp.bfloat16)
    joined[...] = dot(normed[...], w_qkv[...])
    pair = 2 * HEAD_DIM
    for first in range(0, inner + kv_width, pair):
        block = joined[:, first : first + pair]
        qkv[:, first : first + pair] = (
            block * cosine[...] + turned(block, signed[...])
        ).astype(jnp.bfloat16)
    qkv[:, inner + kv_width :] = joined[:, inner + kv_width :].astype(jnp.bfloat16)
    shape = (group * length, length)
    row = lax.broadcasted_iota(jnp.int32, shape, 0) % length
    causal = row >= lax.broadcasted_iota(jnp.int32, shape, 1)
    for kv in range(KV_HEADS):
        start = inner + kv * HEAD_DIM
        key = qkv[:, start : start + HEAD_DIM]
        value = qkv[:, start + kv_width : start + kv_width + HEAD_DIM]
        scores = dot(heads(qkv, group, kv), key, NT) * HEAD_DIM ** (-0.5)
        weights = jnp.where(causal, jnp.exp(scores), 0.0)
        rounded = (weights * (1.0 / jnp.sum(weights, axis=1, keepdims=True))).astype(jnp.bfloat16)
        probs[kv] = rounded
        mixed = dot(rounded, value).astype(jnp.bfloat16)
        for h in range(group):
            first = (kv * group + h) * HEAD_DIM
            context[:, first : first + HEAD_DIM] = mixed[h * length : (h + 1) * length]
    out[...] = (x[...].astype(jnp.float32) + dot(context[...], w_out[...], NT)).astype(jnp.bfloat16)


def backward_kernel(
    grad_in, x, gain, w_qkv, w_out, cosine, signed, qkv, probs, grad_x, grad_joined, wide, grad_ctx
):
    length = x.shape[0]
    group, inner, kv_width = HEADS // KV_HEADS, HEADS * HEAD_DIM, KV_HEADS * HEAD_DIM
    grad_ctx[...] = dot(grad_in[...], w_out[...]).astype(jnp.bfloat16)
    for kv in range(KV_HEADS):
        start = inner + kv * HEAD_DIM
        key = qkv[:, start : start + HEAD_DIM]
        value = qkv[:, start + kv_width : start + kv_width + HEAD_DIM]
        from_ctx = heads(grad_ctx, group, kv)
        kept = probs[kv].astype(jnp.float32)
        grad_probs = dot(from_ctx, value, NT)
        wide[:, start + kv_width : start + kv_width + HEAD_DIM] = dot(probs[kv], from_ctx, TN)
        centred = grad_probs - jnp.sum(grad_probs * kept, axis=1, keepdims=True)
        grad_scores = (kept * centred * HEAD_DIM ** (-0.5)).astype(jnp.bfloat16)
        grad_query = dot(grad_scores, key)
        for h in range(group):
            first = (kv * group + h) * HEAD_DIM
            wide[:, first : first + HEAD_DIM] = grad_query[h * length : (h + 1) * length]
        wide[:, start : start + HEAD_DIM] = dot(grad_scores, heads(qkv, group, kv), TN)
    pair = 2 * HEAD_DIM
    for first in range(0, inner + kv_width, pair):
        block = wide[:, first : first + pair]
        grad_joined[:, first : first + pair] = (
            block * cosine[...] - turned(block, signed[...])
        ).astype(jnp.bfloat16)
    grad_joined[:, inner + kv_width :] = wide[:, inner + kv_width :].astype(jnp.bfloat16)
    values = x[...].astype(jnp.float32)
    scale_inv = norm_scale(values)
    scaled = dot(grad_joined[...], w_qkv[...], NT) * gain[...]
    centre = scale_inv**3 * jnp.mean(scaled * values, axis=1, keepdims=True)
    total = scale_inv * scaled - values * centre + grad_in[...].astype(jnp.float32)
    grad_x[...] = total.astype(jnp.bfloat16)


def local_call(kernel, flops, results, scratch, operands):
    moved = sum(array.size * array.dtype.itemsize for array in operands)
    return pl.pallas_call(
        kernel,
        out_shape=[jax.ShapeDtypeStruct(shape, jnp.bfloat16) for shape in results],
        in_specs=[pl.BlockSpec(memory_space=pltpu.VMEM)] * len(operands),
        out_specs=[pl.BlockSpec(memory_space=pltpu.VMEM)] * len(results),
        scratch_shapes=scratch,
        cost_estimate=pl.CostEstimate(flops=flops, bytes_accessed=moved, transcendentals=0),
        compiler_params=pltpu.CompilerParams(vmem_limit_bytes=24 * 1024 * 1024),
    )(*operands)


def run_forward(x, weights):
    length, width = x.shape
    columns, inner = weights[1].shape[1], weights[2].shape[1]
    probs = (KV_HEADS, HEADS // KV_HEADS * length, length)
    results = [(length, width), (length, width), (length, columns), probs, (length, inner)]
    scratch = [pltpu.VMEM((length, columns), jnp.float32)]
    flops = 2 * length * width * (columns + inner)
    out, normed, qkv, probs, context = local_call(
        forward_kernel, flops, results, scratch, (x, *weights)
    )
    return (out, x, normed, qkv, probs, context)


def run_backward(grad_in, x, qkv, probs, weights):
    length, width = x.shape
    columns, inner = weights[1].shape[1], weights[2].shape[1]
    scratch = [pltpu.VMEM((length, columns), jnp.float32), pltpu.VMEM((length, inner), jnp.bfloat16)]
    flops = 2 * length * width * (columns + inner)
    results = [(length, width), (length, columns)]
    return local_call(
        backward_kernel, flops, results, scratch, (grad_in, x, *weights, qkv, probs)
    )


def pick(first, own, other):
    return jax.tree.map(lambda left, right: jnp.where(first, left, right), own, other)


def two_sections(inputs, cotangent, gains, w_qkv, w_out):
    first = lax.axis_index("pp") == 0
    full_qkv, full_out, full_gain = gather(w_qkv[0], w_out[0], gains[0])
    micro_count, length, width = inputs.shape
    cosine, sine = rope_tables(length)
    half = HEAD_DIM // 2
    cosine = jnp.concatenate([cosine, cosine], axis=1)
    signed = jnp.concatenate([-sine[:, :half], sine[:, half:]] * 2, axis=1)
    weights = (full_gain.astype(jnp.float32)[None], full_qkv, full_out, cosine, signed)
    early, sent = [], []
    for micro in range(micro_count):
        early.append(run_forward(inputs[micro], weights))
        sent.append(shifted(early[-1][0], "pp", 1))
    late, back = [], []
    for micro in range(micro_count):
        arrived = sent[micro]
        if micro > 0:
            arrived, grad_x = lax.optimization_barrier((arrived, grad_x))
            back.append(shifted(grad_x, "pp", -1))
        late.append(run_forward(arrived, weights))
        _, x, _, qkv, probs, _ = late[-1]
        grad_x = run_backward(cotangent[micro], x, qkv, probs, weights)[0]
    back.append(shifted(grad_x, "pp", -1))
    kept = []
    for micro in range(micro_count):
        out, x, normed, qkv, probs, context = pick(first, early[micro], late[micro])
        grad_in = jnp.where(first, back[micro], cotangent[micro])
        grad_joined = run_backward(grad_in, x, qkv, probs, weights)[1]
        kept.append((out, normed, grad_joined, grad_in, context))
    outputs, normed, joined, incoming, context = zip(*kept)
    return finish(outputs, normed, joined, incoming, context, gains, w_qkv)


def finish(outputs, normed, joined, incoming, context, gains, w_qkv):
    pieces = (jnp.concatenate(piece, axis=0) for piece in (normed, joined, incoming, context))
    grad_qkv, grad_out = reduce_terms(*pieces)
    grad_gain = jnp.sum(grad_qkv * w_qkv[0].astype(jnp.float32), axis=1) / gains[0].astype(
        jnp.float32
    )
    return (jnp.stack(outputs)[None], grad_qkv[None], grad_out[None], grad_gain[None])


def solution(mesh):
    return jax.shard_map(
        two_sections if mesh.shape["pp"] == 2 else staged,
        mesh=mesh,
        in_specs=(
            P(None, "fsdp", None),
            P(None, "fsdp", None),
            P("pp", "fsdp"),
            P("pp", "fsdp", None),
            P("pp", "fsdp", None),
        ),
        out_specs=(
            P("pp", None, "fsdp", None),
            P("pp", "fsdp", None),
            P("pp", "fsdp", None),
            P("pp", "fsdp"),
        ),
        check_vma=False,
    )
```

```python
import functools

import jax
import jax.numpy as jnp
from jax import lax
from jax.experimental import pallas as pl
from jax.experimental.pallas import tpu as pltpu
from jax.sharding import PartitionSpec as P

HEADS = 16
KV_HEADS = 4
HEAD_DIM = 64
MESH = pl.DeviceIdType.MESH
PIECES = 4


def shifted(value, axis, steps):
    count = lax.axis_size(axis)
    leading, last = (max(0, -steps), min(count, count - steps))
    return lax.ppermute(value, axis, [(source, source + steps) for source in range(leading, last)])


def mix(form, left, right):
    return jnp.einsum(form, left, right, preferred_element_type=jnp.float32)


def rope_tables(length):
    positions = jnp.arange(length, dtype=jnp.float32)
    freqs = 500000.0 ** (-jnp.arange(HEAD_DIM // 2, dtype=jnp.float32) * 2.0 / HEAD_DIM)
    angles = positions[:, None] * freqs[None, :]
    cosine = jnp.concatenate([jnp.cos(angles), jnp.cos(angles)], axis=1)
    sine = jnp.concatenate([jnp.sin(angles), jnp.sin(angles)], axis=1)
    return (cosine, sine)


def rotate_half(values):
    first = values[..., : HEAD_DIM // 2]
    second = values[..., HEAD_DIM // 2 :]
    return jnp.concatenate([-second, first], axis=-1)


def apply_rope(values, cosine, sine):
    return values * cosine[:, None, :] + rotate_half(values) * sine[:, None, :]


def undo_rope(grads, cosine, sine):
    return grads * cosine[:, None, :] - rotate_half(grads * sine[:, None, :])


def layer_forward(layer_in, gain, w_qkv, w_out, cosine, sine):
    length = layer_in.shape[0]
    group = HEADS // KV_HEADS
    inner = HEADS * HEAD_DIM
    kv_width = KV_HEADS * HEAD_DIM
    values = layer_in.astype(jnp.float32)
    scale_inv = lax.rsqrt(jnp.mean(values * values, axis=-1, keepdims=True) + 1e-05)
    normed = (values * scale_inv * gain.astype(jnp.float32)).astype(jnp.bfloat16)
    joined = jnp.dot(normed, w_qkv, preferred_element_type=jnp.float32)
    queries = apply_rope(joined[:, :inner].reshape(length, HEADS, HEAD_DIM), cosine, sine).astype(
        jnp.bfloat16
    )
    keys = apply_rope(
        joined[:, inner : inner + kv_width].reshape(length, KV_HEADS, HEAD_DIM), cosine, sine
    ).astype(jnp.bfloat16)
    values_v = (
        joined[:, inner + kv_width :].reshape(length, KV_HEADS, HEAD_DIM).astype(jnp.bfloat16)
    )
    grouped = queries.reshape(length, KV_HEADS, group, HEAD_DIM)
    scores = mix("skgh,tkh->kgst", grouped, keys) * HEAD_DIM ** (-0.5)
    causal = jnp.arange(length)[:, None] >= jnp.arange(length)[None, :]
    weights = jnp.where(causal, jnp.exp(scores), 0.0)
    probs = (weights / jnp.sum(weights, axis=-1, keepdims=True)).astype(jnp.bfloat16)
    context = mix("kgst,tkh->skgh", probs, values_v).reshape(length, inner).astype(jnp.bfloat16)
    mixed = values + mix("sc,dc->sd", context, w_out)
    saved = (values, scale_inv, normed, grouped, keys, values_v, probs, context)
    return (mixed.astype(jnp.bfloat16), saved)


def layer_backward(grad_in, saved, gain, w_qkv, w_out, cosine, sine):
    values, scale_inv, normed, grouped, keys, values_v, probs, context = saved
    length = grad_in.shape[0]
    group = HEADS // KV_HEADS
    inner = HEADS * HEAD_DIM
    kv_width = KV_HEADS * HEAD_DIM
    grad_ctx = jnp.dot(grad_in, w_out, preferred_element_type=jnp.float32).astype(jnp.bfloat16)
    grad_ctx = grad_ctx.reshape(length, KV_HEADS, group, HEAD_DIM)
    grad_probs = mix("skgh,tkh->kgst", grad_ctx, values_v)
    grad_values = mix("kgst,skgh->tkh", probs, grad_ctx)
    probs_wide = probs.astype(jnp.float32)
    grad_scores = probs_wide * (
        grad_probs - jnp.sum(grad_probs * probs_wide, axis=-1, keepdims=True)
    )
    grad_scores = (grad_scores * HEAD_DIM ** (-0.5)).astype(jnp.bfloat16)
    grad_queries = mix("kgst,tkh->skgh", grad_scores, keys).reshape(length, HEADS, HEAD_DIM)
    grad_keys = mix("kgst,skgh->tkh", grad_scores, grouped)
    grad_joined = jnp.concatenate(
        [
            undo_rope(grad_queries, cosine, sine).reshape(length, inner),
            undo_rope(grad_keys, cosine, sine).reshape(length, kv_width),
            grad_values.reshape(length, kv_width),
        ],
        axis=1,
    ).astype(jnp.bfloat16)
    grad_normed = mix("sj,dj->sd", grad_joined, w_qkv)
    scaled = grad_normed * gain.astype(jnp.float32)
    grad_x = scale_inv * scaled - values * scale_inv**3 * jnp.mean(
        scaled * values, axis=-1, keepdims=True
    )
    grad_x = grad_x + grad_in.astype(jnp.float32)
    return (grad_x.astype(jnp.bfloat16), grad_joined)


def staged(inputs, cotangent, gains, w_qkv, w_out):
    section_count = lax.axis_size("pp")
    section_index = lax.axis_index("pp")
    full_qkv, full_out, full_gain = (
        lax.all_gather(w_qkv[0], "fsdp", axis=0, tiled=True),
        lax.all_gather(w_out[0], "fsdp", axis=0, tiled=True),
        lax.all_gather(gains[0], "fsdp", axis=0, tiled=True),
    )
    micro_count, length, width = inputs.shape
    joined_width = full_qkv.shape[1]
    inner = full_out.shape[1]
    tick_count = micro_count + section_count - 1
    last_section = section_count - 1
    cosine, sine = rope_tables(length)

    def forward_tick(carry, tick):
        received, saved_in, outputs = carry
        slot = tick - section_index
        valid = jnp.logical_and(slot >= 0, slot < micro_count)
        slot_index = jnp.clip(slot, 0, micro_count - 1)
        first_in = lax.dynamic_index_in_dim(inputs, slot_index, 0, keepdims=False)
        layer_in = jnp.where(section_index == 0, first_in, received)

        def forward_run_layer(operands):
            current, kept_in, kept_out = operands
            layer_out = layer_forward(current, full_gain, full_qkv, full_out, cosine, sine)[0]
            kept_in = lax.dynamic_update_index_in_dim(kept_in, current, slot_index, 0)
            kept_out = lax.dynamic_update_index_in_dim(kept_out, layer_out, slot_index, 0)
            return (layer_out, kept_in, kept_out)

        def forward_skip_layer(operands):
            current, kept_in, kept_out = operands
            return (jnp.zeros_like(current), kept_in, kept_out)

        layer_out, saved_in, outputs = lax.cond(
            valid, forward_run_layer, forward_skip_layer, (layer_in, saved_in, outputs)
        )
        received = shifted(layer_out, "pp", 1)
        return ((received, saved_in, outputs), None)

    blank = jnp.zeros((micro_count, length, width), jnp.bfloat16)
    start_carry = (jnp.zeros((length, width), jnp.bfloat16), blank, blank)
    (_, saved_in, outputs), _ = lax.scan(forward_tick, start_carry, jnp.arange(tick_count))
    extra = (
        blank,
        jnp.zeros((micro_count, length, inner), jnp.bfloat16),
        jnp.zeros((micro_count, length, joined_width), jnp.bfloat16),
        blank,
    )

    def backward_tick(carry, tick):
        received, kept = carry
        slot = tick - (last_section - section_index)
        valid = jnp.logical_and(slot >= 0, slot < micro_count)
        slot_index = jnp.clip(slot, 0, micro_count - 1)
        last_in = lax.dynamic_index_in_dim(cotangent, slot_index, 0, keepdims=False)
        grad_in = jnp.where(section_index == last_section, last_in, received)

        def backward_run_layer(operands):
            current, store = operands
            layer_in = lax.dynamic_index_in_dim(saved_in, slot_index, 0, keepdims=False)
            saved = layer_forward(layer_in, full_gain, full_qkv, full_out, cosine, sine)[1]
            grad_x, grad_joined = layer_backward(
                current, saved, full_gain, full_qkv, full_out, cosine, sine
            )
            pieces = (saved[2], saved[7], grad_joined, current)
            store = tuple(
                (
                    lax.dynamic_update_index_in_dim(buffer, piece, slot_index, 0)
                    for buffer, piece in zip(store, pieces)
                )
            )
            return (grad_x, store)

        def backward_skip_layer(operands):
            current, store = operands
            return (jnp.zeros_like(current), store)

        grad_x, kept = lax.cond(valid, backward_run_layer, backward_skip_layer, (grad_in, kept))
        received = shifted(grad_x, "pp", -1)
        return ((received, kept), None)

    (_, extra), _ = lax.scan(
        backward_tick, (jnp.zeros((length, width), jnp.bfloat16), extra), jnp.arange(tick_count)
    )
    normed_all, context_all, joined_all, incoming_all = extra
    summed = lax.psum_scatter(
        jnp.concatenate(
            [
                mix("msd,msj->dj", normed_all, joined_all),
                mix("msd,msc->dc", incoming_all, context_all),
            ],
            axis=1,
        ).astype(jnp.bfloat16),
        "fsdp",
        scatter_dimension=0,
        tiled=True,
    ).astype(jnp.float32)
    grad_qkv = summed[:, :joined_width]
    grad_out = summed[:, joined_width:]
    grad_gain = jnp.sum(grad_qkv * w_qkv[0].astype(jnp.float32), axis=1) / gains[0].astype(
        jnp.float32
    )
    return (outputs[None], grad_qkv[None], grad_out[None], grad_gain[None])


def place(count):
    me = lax.axis_index("fsdp")
    return (count // 4, me // 4, (me // 2) % 2, me % 2)


def at(outer, side, core):
    return (outer * 2 + side) * 2 + core


def remote(source, target, send_sem, recv_sem, device):
    return pltpu.make_async_remote_copy(
        src_ref=source,
        dst_ref=target,
        send_sem=send_sem,
        recv_sem=recv_sem,
        device_id={"fsdp": device},
        device_id_type=MESH,
    )


def greet(outers, outer, side, core):
    barrier = pltpu.get_barrier_semaphore()
    peers = [at((outer + step) % outers, side, core) for step in range(1, outers)]
    peers += [at(outer, 1 - side, core), at(outer, side, 1 - core)]
    for peer in peers:
        pl.semaphore_signal(barrier, inc=1, device_id={"fsdp": peer}, device_id_type=MESH)
    pl.semaphore_wait(barrier, len(peers))


def gather_kernel(
    count, qkv, out, gain, full_qkv, full_out, full_gain, own, z_out, z_in, x_out, x_in, c_out, c_in
):
    outers, outer, side, core = place(count)
    greet(outers, outer, side, core)
    parts = [(gain, full_gain, 0, gain.shape[0])]
    for source, target in ((qkv, full_qkv), (out, full_out)):
        size = source.shape[0] // 2
        parts += [(source, target, k * size, size) for k in range(2)]
    beside, partner = at(outer, 1 - side, core), at(outer, side, 1 - core)

    def rows(part, owner):
        source, target, start, size = part
        first = pl.multiple_of(owner * source.shape[0] + start, 16)
        return target.at[pl.ds(first, size)]

    started, local = [], []

    def send(source, target, send_sem, recv_sem, device):
        copy = remote(source, target, send_sem, recv_sem, device)
        copy.start()
        started.append(copy)

    for j, part in enumerate(parts):
        source, target, start, size = part
        block, spot = source.at[pl.ds(start, size)], rows(part, at(outer, side, core))
        for step in range(1, outers):
            peer = at((outer + step) % outers, side, core)
            send(block, spot, z_out.at[step, j], z_in.at[step, j], peer)
        send(block, spot, x_out.at[0, j], x_in.at[0, j], beside)
        send(block, spot, c_out.at[0, 0, j], c_in.at[0, 0, j], partner)
        copy = pltpu.make_async_copy(block, spot, own.at[j])
        copy.start()
        local.append(copy)
    for j, part in enumerate(parts):
        for step in range(1, outers):
            spot = rows(part, at((outer + outers - step) % outers, side, core))
            remote(spot, spot, z_out.at[step, j], z_in.at[step, j], beside).wait_recv()
            send(spot, spot, x_out.at[step, j], x_in.at[step, j], beside)
            send(spot, spot, c_out.at[0, step, j], c_in.at[0, step, j], partner)
        for step in range(outers):
            spot = rows(part, at((outer + outers - step) % outers, 1 - side, core))
            remote(spot, spot, x_out.at[step, j], x_in.at[step, j], beside).wait_recv()
            send(spot, spot, c_out.at[1, step, j], c_in.at[1, step, j], partner)
    for j, part in enumerate(parts):
        for over in range(2):
            for step in range(outers):
                origin = at(
                    (outer + outers - step) % outers, 1 - side if over else side, 1 - core
                )
                spot = rows(part, origin)
                remote(
                    spot, spot, c_out.at[over, step, j], c_in.at[over, step, j], partner
                ).wait_recv()
    for copy in started:
        copy.wait_send()
    for copy in local:
        copy.wait()


def gather(qkv, out, gain):
    count = lax.axis_size("fsdp")
    outers = count // 4
    gain = jnp.broadcast_to(gain[None], (16, gain.shape[0]))
    sems = [(outers, 5), (outers, 5), (outers, 5), (outers, 5), (2, outers, 5), (2, outers, 5)]
    full_qkv, full_out, full_gain = pl.pallas_call(
        functools.partial(gather_kernel, count),
        out_shape=[
            jax.ShapeDtypeStruct((count * block.shape[0], block.shape[1]), block.dtype)
            for block in (qkv, out, gain)
        ],
        in_specs=[pl.BlockSpec(memory_space=pl.ANY)] * 3,
        out_specs=[pl.BlockSpec(memory_space=pl.ANY)] * 3,
        scratch_shapes=[pltpu.SemaphoreType.DMA((5,))]
        + [pltpu.SemaphoreType.DMA(shape) for shape in sems],
        compiler_params=pltpu.CompilerParams(collective_id=0, has_side_effects=True),
    )(qkv, out, gain)
    return (full_qkv, full_out, full_gain.reshape(count, 16, -1)[:, 0].reshape(-1))


def reduce_kernel(
    count, normed, joined, incoming, context, sum_qkv, sum_out,
    c_buf, own, c_got, x_buf, x_got, z_buf, z_got, c_out, c_in, x_out, x_in, z_out, z_in,
):
    outers, outer, side, core = place(count)
    depth, width = sum_qkv.shape
    beside, partner = at(outer, 1 - side, core), at(outer, side, 1 - core)
    greet(outers, outer, side, core)

    def term(index, target):
        columns = pl.ds(pl.multiple_of(index * depth, depth), depth)
        form = (((0,), (0,)), ((), ()))
        target[:, :width] = lax.dot_general(
            normed[:, columns], joined[...], form, preferred_element_type=jnp.float32
        ).astype(jnp.bfloat16)
        target[:, width:] = lax.dot_general(
            incoming[:, columns], context[...], form, preferred_element_type=jnp.float32
        ).astype(jnp.bfloat16)

    def to_core(k):
        return remote(c_buf.at[k], c_got.at[k], c_out.at[k], c_in.at[k], partner)

    part = (width + context.shape[1]) // PIECES

    def cut(p):
        return slice(p * part, (p + 1) * part)

    def to_side(k, p):
        source, target = x_buf.at[k, :, cut(p)], x_got.at[k, :, cut(p)]
        return remote(source, target, x_out.at[k, p], x_in.at[k, p], beside)

    def to_outer(k, p):
        peer = at((outer + k + 1) % outers, side, core)
        source, target = z_buf.at[k, :, cut(p)], z_got.at[k, :, cut(p)]
        return remote(source, target, z_out.at[k, p], z_in.at[k, p], peer)

    def wide(ref):
        return ref[...].astype(jnp.float32)

    def combine(k):
        to_core(k).wait_recv()
        both = (wide(own.at[k]) + wide(c_got.at[k])).astype(jnp.bfloat16)

        @pl.when(k < outers)
        def _():
            x_buf[k % outers] = both
            for p in range(PIECES):
                to_side(k % outers, p).start()

        @pl.when(k >= outers)
        def _():
            own[k] = both

    def one(k, carry):
        where = (outer + k + 1) % outers
        over = k // outers
        there = over * side + (1 - over) * (1 - side)
        term(at(where, there, 1 - core), c_buf.at[k])
        to_core(k).start()
        term(at(where, there, core), own.at[k])

        @pl.when(k > 0)
        def _():
            combine(k - 1)

        return carry

    lax.fori_loop(0, 2 * outers, one, 0)
    combine(2 * outers - 1)

    def two(k, carry):
        for p in range(PIECES):
            to_side(k, p).wait_recv()
            z_buf[k, :, cut(p)] = (
                own[outers + k, :, cut(p)].astype(jnp.float32)
                + x_got[k, :, cut(p)].astype(jnp.float32)
            ).astype(jnp.bfloat16)
            to_outer(k, p).start()
        return carry

    lax.fori_loop(0, outers - 1, two, 0)
    last = outers - 1
    for p in range(PIECES):
        to_side(last, p).wait_recv()
        for k in range(last):
            to_outer(k, p).wait_recv()
    total = wide(own.at[outers + last]) + wide(x_got.at[last])
    for k in range(last):
        total += wide(z_got.at[k])
    sum_qkv[...] = total[:, :width]
    sum_out[...] = total[:, width:]

    for k in range(2 * outers):
        to_core(k).wait_send()
    for p in range(PIECES):
        for k in range(outers):
            to_side(k, p).wait_send()
        for k in range(last):
            to_outer(k, p).wait_send()


def reduce_terms(normed, joined, incoming, context):
    count = lax.axis_size("fsdp")
    outers = count // 4
    tokens, width = normed.shape
    depth = width // count
    columns = joined.shape[1] + context.shape[1]

    def slots(number):
        return pltpu.VMEM((number, depth, columns), jnp.bfloat16)

    numbers = (2 * outers, 2 * outers, 2 * outers, outers, outers, outers - 1, outers - 1)
    sems = [(2 * outers,)] * 2 + [(outers, PIECES)] * 2 + [(outers - 1, PIECES)] * 2
    return pl.pallas_call(
        functools.partial(reduce_kernel, count),
        out_shape=[
            jax.ShapeDtypeStruct((depth, piece.shape[1]), jnp.float32) for piece in (joined, context)
        ],
        in_specs=[pl.BlockSpec(memory_space=pltpu.VMEM)] * 4,
        out_specs=[pl.BlockSpec(memory_space=pltpu.VMEM)] * 2,
        scratch_shapes=[slots(number) for number in numbers]
        + [pltpu.SemaphoreType.DMA(shape) for shape in sems],
        compiler_params=pltpu.CompilerParams(
            collective_id=1, has_side_effects=True, vmem_limit_bytes=48 * 1024 * 1024
        ),
    )(normed, joined, incoming, context)


NT = (((1,), (1,)), ((), ()))
TN = (((0,), (0,)), ((), ()))


def dot(left, right, form=(((1,), (0,)), ((), ()))):
    return lax.dot_general(left, right, form, preferred_element_type=jnp.float32)


def turned(values, signed):
    lane = lax.broadcasted_iota(jnp.int32, values.shape, 1) % HEAD_DIM
    ahead = pltpu.roll(values, 2 * HEAD_DIM - HEAD_DIM // 2, 1)
    behind = pltpu.roll(values, HEAD_DIM // 2, 1)
    return jnp.where(lane < HEAD_DIM // 2, ahead, behind) * signed


def heads(ref, group, kv):
    first = kv * group
    return jnp.concatenate(
        [ref[:, h * HEAD_DIM : (h + 1) * HEAD_DIM] for h in range(first, first + group)], axis=0
    )


def norm_scale(values):
    return lax.rsqrt(jnp.mean(values * values, axis=1, keepdims=True) + 1e-05)


def forward_kernel(x, gain, w_qkv, w_out, cosine, signed, out, normed, qkv, probs, context, joined):
    length = x.shape[0]
    group, inner, kv_width = HEADS // KV_HEADS, HEADS * HEAD_DIM, KV_HEADS * HEAD_DIM
    values = x[...].astype(jnp.float32)
    normed[...] = (values * norm_scale(values) * gain[...]).astype(jnp.bfloat16)
    joined[...] = dot(normed[...], w_qkv[...])
    pair = 2 * HEAD_DIM
    for first in range(0, inner + kv_width, pair):
        block = joined[:, first : first + pair]
        qkv[:, first : first + pair] = (
            block * cosine[...] + turned(block, signed[...])
        ).astype(jnp.bfloat16)
    qkv[:, inner + kv_width :] = joined[:, inner + kv_width :].astype(jnp.bfloat16)
    shape = (group * length, length)
    row = lax.broadcasted_iota(jnp.int32, shape, 0) % length
    causal = row >= lax.broadcasted_iota(jnp.int32, shape, 1)
    for kv in range(KV_HEADS):
        start = inner + kv * HEAD_DIM
        key = qkv[:, start : start + HEAD_DIM]
        value = qkv[:, start + kv_width : start + kv_width + HEAD_DIM]
        scores = dot(heads(qkv, group, kv), key, NT) * HEAD_DIM ** (-0.5)
        weights = jnp.where(causal, jnp.exp(scores), 0.0)
        rounded = (weights * (1.0 / jnp.sum(weights, axis=1, keepdims=True))).astype(jnp.bfloat16)
        probs[kv] = rounded
        mixed = dot(rounded, value).astype(jnp.bfloat16)
        for h in range(group):
            first = (kv * group + h) * HEAD_DIM
            context[:, first : first + HEAD_DIM] = mixed[h * length : (h + 1) * length]
    out[...] = (x[...].astype(jnp.float32) + dot(context[...], w_out[...], NT)).astype(jnp.bfloat16)


def backward_kernel(
    grad_in, x, gain, w_qkv, w_out, cosine, signed, qkv, probs, grad_x, grad_joined, wide, grad_ctx
):
    length = x.shape[0]
    group, inner, kv_width = HEADS // KV_HEADS, HEADS * HEAD_DIM, KV_HEADS * HEAD_DIM
    grad_ctx[...] = dot(grad_in[...], w_out[...]).astype(jnp.bfloat16)
    for kv in range(KV_HEADS):
        start = inner + kv * HEAD_DIM
        key = qkv[:, start : start + HEAD_DIM]
        value = qkv[:, start + kv_width : start + kv_width + HEAD_DIM]
        from_ctx = heads(grad_ctx, group, kv)
        kept = probs[kv].astype(jnp.float32)
        grad_probs = dot(from_ctx, value, NT)
        wide[:, start + kv_width : start + kv_width + HEAD_DIM] = dot(probs[kv], from_ctx, TN)
        centred = grad_probs - jnp.sum(grad_probs * kept, axis=1, keepdims=True)
        grad_scores = (kept * centred * HEAD_DIM ** (-0.5)).astype(jnp.bfloat16)
        grad_query = dot(grad_scores, key)
        for h in range(group):
            first = (kv * group + h) * HEAD_DIM
            wide[:, first : first + HEAD_DIM] = grad_query[h * length : (h + 1) * length]
        wide[:, start : start + HEAD_DIM] = dot(grad_scores, heads(qkv, group, kv), TN)
    pair = 2 * HEAD_DIM
    for first in range(0, inner + kv_width, pair):
        block = wide[:, first : first + pair]
        grad_joined[:, first : first + pair] = (
            block * cosine[...] - turned(block, signed[...])
        ).astype(jnp.bfloat16)
    grad_joined[:, inner + kv_width :] = wide[:, inner + kv_width :].astype(jnp.bfloat16)
    values = x[...].astype(jnp.float32)
    scale_inv = norm_scale(values)
    scaled = dot(grad_joined[...], w_qkv[...], NT) * gain[...]
    centre = scale_inv**3 * jnp.mean(scaled * values, axis=1, keepdims=True)
    total = scale_inv * scaled - values * centre + grad_in[...].astype(jnp.float32)
    grad_x[...] = total.astype(jnp.bfloat16)


def local_call(kernel, flops, results, scratch, operands):
    moved = sum(array.size * array.dtype.itemsize for array in operands)
    return pl.pallas_call(
        kernel,
        out_shape=[jax.ShapeDtypeStruct(shape, jnp.bfloat16) for shape in results],
        in_specs=[pl.BlockSpec(memory_space=pltpu.VMEM)] * len(operands),
        out_specs=[pl.BlockSpec(memory_space=pltpu.VMEM)] * len(results),
        scratch_shapes=scratch,
        cost_estimate=pl.CostEstimate(flops=flops, bytes_accessed=moved, transcendentals=0),
        compiler_params=pltpu.CompilerParams(vmem_limit_bytes=24 * 1024 * 1024),
    )(*operands)


def run_forward(x, weights):
    length, width = x.shape
    columns, inner = weights[1].shape[1], weights[2].shape[1]
    probs = (KV_HEADS, HEADS // KV_HEADS * length, length)
    results = [(length, width), (length, width), (length, columns), probs, (length, inner)]
    scratch = [pltpu.VMEM((length, columns), jnp.float32)]
    flops = 2 * length * width * (columns + inner)
    out, normed, qkv, probs, context = local_call(
        forward_kernel, flops, results, scratch, (x, *weights)
    )
    return (out, x, normed, qkv, probs, context)


def run_backward(grad_in, x, qkv, probs, weights):
    length, width = x.shape
    columns, inner = weights[1].shape[1], weights[2].shape[1]
    scratch = [pltpu.VMEM((length, columns), jnp.float32), pltpu.VMEM((length, inner), jnp.bfloat16)]
    flops = 2 * length * width * (columns + inner)
    results = [(length, width), (length, columns)]
    return local_call(
        backward_kernel, flops, results, scratch, (grad_in, x, *weights, qkv, probs)
    )


def pick(first, own, other):
    return jax.tree.map(lambda left, right: jnp.where(first, left, right), own, other)


def two_sections(inputs, cotangent, gains, w_qkv, w_out):
    first = lax.axis_index("pp") == 0
    full_qkv, full_out, full_gain = gather(w_qkv[0], w_out[0], gains[0])
    micro_count, length, width = inputs.shape
    cosine, sine = rope_tables(length)
    half = HEAD_DIM // 2
    cosine = jnp.concatenate([cosine, cosine], axis=1)
    signed = jnp.concatenate([-sine[:, :half], sine[:, half:]] * 2, axis=1)
    weights = (full_gain.astype(jnp.float32)[None], full_qkv, full_out, cosine, signed)
    early, sent = [], []
    for micro in range(micro_count):
        early.append(run_forward(inputs[micro], weights))
        sent.append(shifted(early[-1][0], "pp", 1))
    late, back = [], []
    for micro in range(micro_count):
        arrived = sent[micro]
        if micro > 0:
            arrived, grad_x = lax.optimization_barrier((arrived, grad_x))
            back.append(shifted(grad_x, "pp", -1))
        late.append(run_forward(arrived, weights))
        _, x, _, qkv, probs, _ = late[-1]
        grad_x = run_backward(cotangent[micro], x, qkv, probs, weights)[0]
    back.append(shifted(grad_x, "pp", -1))
    kept = []
    for micro in range(micro_count):
        out, x, normed, qkv, probs, context = pick(first, early[micro], late[micro])
        grad_in = jnp.where(first, back[micro], cotangent[micro])
        grad_joined = run_backward(grad_in, x, qkv, probs, weights)[1]
        kept.append((out, normed, grad_joined, grad_in, context))
    outputs, normed, joined, incoming, context = zip(*kept)
    return finish(outputs, normed, joined, incoming, context, gains, w_qkv)


def finish(outputs, normed, joined, incoming, context, gains, w_qkv):
    pieces = (jnp.concatenate(piece, axis=0) for piece in (normed, joined, incoming, context))
    grad_qkv, grad_out = reduce_terms(*pieces)
    grad_gain = jnp.sum(grad_qkv * w_qkv[0].astype(jnp.float32), axis=1) / gains[0].astype(
        jnp.float32
    )
    return (jnp.stack(outputs)[None], grad_qkv[None], grad_out[None], grad_gain[None])


def solution(mesh):
    return jax.shard_map(
        two_sections if mesh.shape["pp"] == 2 else staged,
        mesh=mesh,
        in_specs=(
            P(None, "fsdp", None),
            P(None, "fsdp", None),
            P("pp", "fsdp"),
            P("pp", "fsdp", None),
            P("pp", "fsdp", None),
        ),
        out_specs=(
            P("pp", None, "fsdp", None),
            P("pp", "fsdp", None),
            P("pp", "fsdp", None),
            P("pp", "fsdp"),
        ),
        check_vma=False,
    )
```
